256 devices in a mesh: ctx: 32 (over y, x, core), tp: 4 (over z_lo), pool: 2 (over z_hi).
Axes of the slice: x: 4, y: 4, z: 8 (z_hi: 2, z_lo: 4; z = z_hi * 4 + z_lo), core: 2. Of those that a mesh axis runs over, the one named last changes fastest.
Arguments:
- stretch_query: bfloat16 [512, 8192], P('ctx', ('tp', 'pool')), may hold values from -9 to 9
- stretch_key_value: bfloat16 [2, 512, 1024], P(None, 'ctx', ('tp', 'pool')), may hold values from -6 to 6
- cache_kv: bfloat16 [2, 65536, 1024], P(None, 'ctx', ('tp', 'pool')), may hold values from -6 to 6
- stretch_offset: int32 [1], replicated, may hold values from 16384 to 65536
- page_table: int32 [64], replicated, may hold values from 0 to 63, each once
- decode_fresh_query: bfloat16 [128, 2, 8192], P(('ctx', 'pool'), None, 'tp'), may hold values from -9 to 9
- decode_fresh_key_value: bfloat16 [2, 128, 2, 1024], P(None, ('ctx', 'pool'), None, 'tp'), may hold values from -6 to 6
- decode_row_cache: bfloat16 [2, 128, 1024, 1024], P(None, ('ctx', 'pool'), None, 'tp'), may hold values from -6 to 6
- row_lengths: int32 [128], P(('ctx', 'pool')), may hold values from 1 to 1024, 65536 in all
Outputs:
- prefill_context: bfloat16 [512, 8192], P('ctx', ('tp', 'pool'))
- decode_context: bfloat16 [128, 2, 8192], P(('ctx', 'pool'), None, 'tp')
- group_page_slots: bfloat16 [2, 512, 1024], P(None, ('ctx', 'pool'), 'tp')
The draws below stay inside these ranges and needn't reach their ends.
All inputs are finite; a program needn't handle non-finite values. No bound on the sum of `row_lengths` on one device may be relied on, other than what follows from the above.
Results may differ from the reference program's by a relative error of at most 0.0075.
Values may be sent and summed in bfloat16 or wider, within the bound.
No kernel may reach another device: no remote copies, remote signals or barrier semaphores. Data moves between devices by JAX's collectives and lax.ppermute only.
A program may use at most 192 MiB of HBM per device.

```python
import math
import jax
import jax.numpy as jnp
import numpy as np
from jax import lax

QUERY_HEADS = 64
KEY_VALUE_HEADS = 8
HEAD_SIZE = 128
ROW_CAPACITY = 1024
PAGE_TOKENS = 8
DECODE_GROUPS = 64
STRETCH_TOKENS = 512
CACHED_POSITIONS = 65536
DECODE_ROWS = 128


def clipped_pages(key, shape):
    return jax.random.truncated_normal(key, -6.0, 6.0, shape, jnp.float32)


def wide_queries(key, shape):
    return 2.5 * jax.random.truncated_normal(key, -3.6, 3.6, shape, jnp.float32)


def draw_stretch_query(key, part):
    key = jax.random.fold_in(key, 1)
    value_rows = wide_queries(key, (STRETCH_TOKENS, QUERY_HEADS * HEAD_SIZE))
    return value_rows.astype(jnp.bfloat16)


def draw_cache_kv(key, part):
    key = jax.random.fold_in(key, 2)
    value_rows = clipped_pages(key, (2, CACHED_POSITIONS, KEY_VALUE_HEADS * HEAD_SIZE))
    return value_rows.astype(jnp.bfloat16)


def draw_decode_fresh_query(key, part):
    key = jax.random.fold_in(key, 3)
    value_rows = wide_queries(key, (DECODE_ROWS, 2, QUERY_HEADS * HEAD_SIZE))
    return value_rows.astype(jnp.bfloat16)


def draw_decode_fresh_key_value(key, part):
    key = jax.random.fold_in(key, 4)
    value_rows = clipped_pages(key, (2, DECODE_ROWS, 2, KEY_VALUE_HEADS * HEAD_SIZE))
    return value_rows.astype(jnp.bfloat16)


def draw_decode_row_cache(key, part):
    key = jax.random.fold_in(key, 5)
    value_rows = clipped_pages(key, (2, DECODE_ROWS, ROW_CAPACITY, KEY_VALUE_HEADS * HEAD_SIZE))
    return value_rows.astype(jnp.bfloat16)


def level_of(own_key, shape, shards, smallest, largest):
    gain, own = 1.0, jax.random.fold_in(own_key, 6)
    for axis_at, parts in shards:
        steps = jnp.exp(jax.random.uniform(jax.random.fold_in(own, axis_at), (parts,), jnp.float32, smallest / len(shards), largest / len(shards)))
        gain = gain * jnp.repeat(steps, shape[axis_at] // parts).reshape([-1 if axis == axis_at else 1 for axis in range(len(shape))])
    return gain


def split_up(number_of, total, most, slope):
    portions = [(1 << 20) // math.isqrt(rank ** slope) + 1 for rank in range(2, number_of + 1)]
    rest, holding = total - most - (number_of - 1), [1] * (number_of - 1)
    while rest > 0:
        movable = [i for i in range(number_of - 1) if holding[i] < most]
        pool, budget = sum([portions[i] for i in movable]), rest
        for i in movable:
            more = min(most - holding[i], max(1, budget * portions[i] // pool), rest)
            holding[i] = holding[i] + more
            rest = rest - more
    return np.array([most] + holding)


def ragged_sizes(stream_key, count, total, most, skew):
    if count == 2:
        one = jax.random.randint(stream_key, (), max(1, total - most), min(most, total - 1) + 1)
        return jnp.stack([one, total - one])
    tallies = jnp.asarray(split_up(count, total, most, skew), jnp.int32)
    pairs = (count - 1) // 2
    giver, taker = tallies[1:1 + 2 * pairs:2], tallies[2:2 + 2 * pairs:2]
    room = jnp.minimum(giver - 1, most - taker)
    passed = jax.random.randint(jax.random.fold_in(stream_key, 1), (pairs,), 0, 1 << 20) % (room + 1)
    tallies = tallies.at[1:1 + 2 * pairs:2].set(giver - passed).at[2:2 + 2 * pairs:2].set(taker + passed)
    return tallies[jax.random.permutation(jax.random.fold_in(stream_key, 2), count)]


def bell_draw(key, dims, spread, bound, cuts=(), kind=jnp.bfloat16):
    values = jax.random.normal(key, dims, jnp.float32) * spread
    if len(cuts) > 0:
        values = level_of(key, dims, cuts, -0.22, 0.18) * values
    return jnp.clip(values, min=-bound, max=bound).astype(kind)


def setup_inputs(seed: int = 0) -> dict:
    keys = jax.random.split(jax.random.key(seed), 10)
    return {
        "stretch_query": draw_stretch_query(jax.random.fold_in(keys[9], 71), 0),
        "stretch_key_value": bell_draw(keys[1], (2, STRETCH_TOKENS, KEY_VALUE_HEADS * HEAD_SIZE), 1.0, 6.0, ((1, 32), (2, 8))),
        "cache_kv": draw_cache_kv(jax.random.fold_in(keys[9], 71), 0),
        "stretch_offset": jax.random.randint(keys[3], (1,), CACHED_POSITIONS // 4, CACHED_POSITIONS + 1).astype(jnp.int32),
        "page_table": jax.random.permutation(keys[4], DECODE_GROUPS).astype(jnp.int32),
        "decode_fresh_query": draw_decode_fresh_query(jax.random.fold_in(keys[9], 71), 0),
        "decode_fresh_key_value": draw_decode_fresh_key_value(jax.random.fold_in(keys[9], 71), 0),
        "decode_row_cache": draw_decode_row_cache(jax.random.fold_in(keys[9], 71), 0),
        "row_lengths": ragged_sizes(keys[8], DECODE_ROWS, DECODE_ROWS * ROW_CAPACITY // 2, ROW_CAPACITY, 2).astype(jnp.int32),
    }


def prefill_head(head, stretch_query, stretch_key_value, cache_kv, offset):
    scale = HEAD_SIZE ** -0.5
    group_number = QUERY_HEADS // KEY_VALUE_HEADS
    kv_head = head // group_number
    query_rows = lax.dynamic_slice_in_dim(stretch_query, head * HEAD_SIZE, HEAD_SIZE, 1)
    cached_key_rows = lax.dynamic_slice_in_dim(cache_kv[0], kv_head * HEAD_SIZE, HEAD_SIZE, 1)
    cached_value_rows = lax.dynamic_slice_in_dim(cache_kv[1], kv_head * HEAD_SIZE, HEAD_SIZE, 1)
    near_keys = lax.dynamic_slice_in_dim(stretch_key_value[0], kv_head * HEAD_SIZE, HEAD_SIZE, 1)
    near_vals = lax.dynamic_slice_in_dim(stretch_key_value[1], kv_head * HEAD_SIZE, HEAD_SIZE, 1)
    far_scores = jnp.dot(query_rows, cached_key_rows.T, preferred_element_type=jnp.float32) * scale
    near_scores = jnp.dot(query_rows, near_keys.T, preferred_element_type=jnp.float32) * scale
    far_ok = (jnp.arange(CACHED_POSITIONS, dtype=jnp.int32) < offset)[None, :]
    places = jnp.arange(STRETCH_TOKENS, dtype=jnp.int32)
    near_ok = places[None, :] <= places[:, None]
    far_scores = jnp.where(far_ok, far_scores, -1e30)
    near_scores = jnp.where(near_ok, near_scores, -1e30)
    top = jnp.maximum(jnp.max(far_scores, axis=1), jnp.max(near_scores, axis=1))
    far_probs = jnp.where(far_ok, jnp.exp(far_scores - top[:, None]), 0.0)
    near_probs = jnp.where(near_ok, jnp.exp(near_scores - top[:, None]), 0.0)
    total = jnp.sum(far_probs, axis=1) + jnp.sum(near_probs, axis=1)
    mixed = jnp.dot(far_probs.astype(jnp.bfloat16), cached_value_rows, preferred_element_type=jnp.float32)
    mixed = mixed + jnp.dot(near_probs.astype(jnp.bfloat16), near_vals, preferred_element_type=jnp.float32)
    return (mixed / total[:, None]).astype(jnp.bfloat16)


def decode_row(row_number, decode_fresh_query, decode_fresh_key_value, decode_row_cache, row_lengths):
    scale = HEAD_SIZE ** -0.5
    group_number = QUERY_HEADS // KEY_VALUE_HEADS
    query_rows = decode_fresh_query[row_number].astype(jnp.float32).reshape(2, KEY_VALUE_HEADS, group_number, HEAD_SIZE)
    cached_key_rows = decode_row_cache[0, row_number].astype(jnp.float32).reshape(ROW_CAPACITY, KEY_VALUE_HEADS, HEAD_SIZE)
    cached_value_rows = decode_row_cache[1, row_number].astype(jnp.float32).reshape(ROW_CAPACITY, KEY_VALUE_HEADS, HEAD_SIZE)
    fresh_key_rows = decode_fresh_key_value[0, row_number].astype(jnp.float32).reshape(2, KEY_VALUE_HEADS, HEAD_SIZE)
    fresh_value_rows = decode_fresh_key_value[1, row_number].astype(jnp.float32).reshape(2, KEY_VALUE_HEADS, HEAD_SIZE)
    far_scores = jnp.einsum("tgjd,lgd->gtjl", query_rows, cached_key_rows) * scale
    near_scores = jnp.einsum("tgjd,ugd->gtju", query_rows, fresh_key_rows) * scale
    far_ok = (jnp.arange(ROW_CAPACITY, dtype=jnp.int32) < row_lengths[row_number])[None, None, None, :]
    steps = jnp.arange(2, dtype=jnp.int32)
    near_ok = (steps[None, :] <= steps[:, None])[None, :, None, :]
    far_scores = jnp.where(far_ok, far_scores, -1e30)
    near_scores = jnp.where(near_ok, near_scores, -1e30)
    top = jnp.maximum(jnp.max(far_scores, axis=3), jnp.max(near_scores, axis=3))
    far_probs = jnp.where(far_ok, jnp.exp(far_scores - top[..., None]), 0.0)
    near_probs = jnp.where(near_ok, jnp.exp(near_scores - top[..., None]), 0.0)
    total = jnp.sum(far_probs, axis=3) + jnp.sum(near_probs, axis=3)
    far_round = lax.optimization_barrier(far_probs.astype(jnp.bfloat16)).astype(jnp.float32)
    near_round = lax.optimization_barrier(near_probs.astype(jnp.bfloat16)).astype(jnp.float32)
    mixed = jnp.einsum("gtjl,lgd->tgjd", far_round, cached_value_rows)
    mixed = mixed + jnp.einsum("gtju,ugd->tgjd", near_round, fresh_value_rows)
    result = mixed / jnp.transpose(total, (1, 0, 2))[..., None]
    return result.reshape(2, QUERY_HEADS * HEAD_SIZE).astype(jnp.bfloat16)


def reference(stretch_query, stretch_key_value, cache_kv, stretch_offset, page_table, decode_fresh_query, decode_fresh_key_value, decode_row_cache, row_lengths):
    offset = stretch_offset[0]
    heads_out = lax.map(lambda head: prefill_head(head, stretch_query, stretch_key_value, cache_kv, offset), jnp.arange(QUERY_HEADS, dtype=jnp.int32))
    prefill_context = jnp.transpose(heads_out, (1, 0, 2)).reshape(STRETCH_TOKENS, QUERY_HEADS * HEAD_SIZE)
    decode_context = lax.map(lambda row_number: decode_row(row_number, decode_fresh_query, decode_fresh_key_value, decode_row_cache, row_lengths), jnp.arange(DECODE_ROWS, dtype=jnp.int32))
    page_blocks = stretch_key_value.reshape(2, DECODE_GROUPS, PAGE_TOKENS, KEY_VALUE_HEADS * HEAD_SIZE)
    handed_pages = jnp.zeros_like(page_blocks).at[:, page_table].set(page_blocks)
    group_page_slots = handed_pages.reshape(2, STRETCH_TOKENS, KEY_VALUE_HEADS * HEAD_SIZE)
    return (prefill_context, decode_context, group_page_slots)
```

```python
import functools

import jax
import jax.numpy as jnp
from jax import lax
from jax.experimental import pallas as pl
from jax.experimental.pallas import tpu as pltpu
from jax.sharding import PartitionSpec as P

D = 128
SCALE2 = D ** (-0.5) * 1.4426950408889634
NEG = -1e30
SIDE = 4
PIECE = 16
CHUNK = SIDE * PIECE
GROUP = 8
WIDTH = GROUP * D
MSG = WIDTH + D
F32 = jnp.float32
BF16 = jnp.bfloat16
VM = pl.BlockSpec(memory_space=pltpu.VMEM)
SM = pl.BlockSpec(memory_space=pltpu.SMEM)


def place():
    index = lax.axis_index("ctx")
    return index // 8, (index // 2) % 4, index % 2


def moved(value, dy=0, dx=0, dc=0):
    pairs = []
    for y in range(4):
        for x in range(4):
            for c in range(2):
                target = ((y + dy) % 4 * 4 + (x + dx) % 4) * 2 + (c + dc) % 2
                pairs.append(((y * 4 + x) * 2 + c, target))
    return lax.ppermute(value, "ctx", pairs)


def params(mib):
    return pltpu.CompilerParams(vmem_limit_bytes=mib << 20)


def cost(us):
    return pl.CostEstimate(flops=int(us * 1.1e9), bytes_accessed=0, transcendentals=0)


def nt(a, b):
    return lax.dot_general(a, b, (((1,), (1,)), ((), ())), preferred_element_type=F32)


def prepare_kernel(offset, own, other, own_near, other_near, keys, values):
    y, x, c = place()
    span = own.shape[1]
    valid = offset[0] - (y * 4 + x) * 2 * span
    first = jnp.where(c == 0, own[0, 0:16, :].astype(F32), other[0, 0:16, :].astype(F32))[0:1, :]
    for part, (ref, base) in enumerate(((own, c * span), (other, (1 - c) * span))):
        rows = pl.ds(part * span, span)

        @pl.when(valid >= base + span)
        def _():
            keys[rows, :] = ref[0]
            values[rows, 0:D] = ref[1]
            values[rows, D:] = jnp.ones((span, D), BF16)

        @pl.when(valid < base + span)
        def _():
            ok = lax.broadcasted_iota(jnp.int32, (span, D), 0) + base < valid
            keys[rows, :] = jnp.where(ok, ref[0].astype(F32), first).astype(BF16)
            values[rows, 0:D] = jnp.where(ok, ref[1].astype(F32), 0.0).astype(BF16)
            values[rows, D:] = jnp.where(ok, 1.0, 0.0).astype(BF16)

    end = 2 * span
    keys[end : end + 16, :] = own_near[0]
    keys[end + 16 : end + 32, :] = other_near[0]
    keys[end + 32 : end + D, :] = jnp.zeros((D - 32, D), BF16)
    values[end : end + 16, 0:D] = own_near[1]
    values[end + 16 : end + 32, 0:D] = other_near[1]
    values[end + 32 : end + D, 0:D] = jnp.zeros((D - 32, D), BF16)
    values[end : end + D, D:] = jnp.ones((D, D), BF16)


def prepare(offset, own, other, own_near, other_near):
    rows = 2 * own.shape[1] + D
    return pl.pallas_call(
        prepare_kernel,
        out_shape=(
            jax.ShapeDtypeStruct((rows, D), BF16),
            jax.ShapeDtypeStruct((rows, 2 * D), BF16),
        ),
        in_specs=[SM, VM, VM, VM, VM],
        out_specs=(VM, VM),
        compiler_params=params(24),
        cost_estimate=cost(1.5),
    )(offset, own, other, own_near, other_near)


def chunk_kernel(step, block, offset, query, keys, values, out, rows, top, acc, even, odd):
    y, x, c = place()
    n = GROUP * CHUNK
    far = keys.shape[0] - D
    for h in range(GROUP):
        rows[h * CHUNK : (h + 1) * CHUNK, :] = query[:, h * D : (h + 1) * D]
    score = nt(rows[...], keys[far : far + D, :]) * SCALE2
    line = lax.broadcasted_iota(jnp.int32, (n, D), 0) % CHUNK
    lane = lax.broadcasted_iota(jnp.int32, (n, D), 1)
    chunk_y = (y + 4 - step) % 4
    token = line % PIECE
    for d in range(SIDE):
        start = ((chunk_y * 4 + (x + 4 - d) % 4) * 2 + c) * PIECE
        token = token + jnp.where(line // PIECE == d, start, 0)
    chip = (y * 4 + x) * 2
    key = jnp.where(lane < 16, lane + (chip + c) * PIECE, lane - 16 + (chip + 1 - c) * PIECE)
    ok = (key <= token) & (lane < 32)
    score = jnp.where(ok, score, NEG)
    best = jnp.max(score, axis=1, keepdims=True)
    weight = jnp.where(ok, jnp.exp2(score - best), 0.0)
    top[...] = jnp.broadcast_to(best, (n, D))
    acc[...] = jnp.dot(weight.astype(BF16), values[far : far + D, :], preferred_element_type=F32)
    count = far // block

    def scores(b):
        return nt(rows[...], keys[pl.ds(pl.multiple_of(b * block, block), block), :])

    def absorb(ref, b):
        old = top[...]
        s = ref[...]
        new = jnp.maximum(old, jnp.max(s, axis=1, keepdims=True) * SCALE2)
        w = jnp.exp2(s * SCALE2 - new[:, :1]).astype(BF16)
        f = jnp.exp2(old - new)
        v = values[pl.ds(pl.multiple_of(b * block, block), block), :]
        acc[...] = acc[...] * jnp.concatenate([f, f], axis=1) + jnp.dot(
            w, v, preferred_element_type=F32
        )
        top[...] = new

    @pl.when(offset[0] > chip * (far // 2))
    def _():
        even[...] = scores(0)

        @pl.loop(0, count // 2)
        def _(i):
            odd[...] = scores(2 * i + 1)
            absorb(even, 2 * i)
            even[...] = scores(lax.rem(2 * i + 2, count))
            absorb(odd, 2 * i + 1)

    stat = jnp.zeros((CHUNK, D), F32)
    lane = lax.broadcasted_iota(jnp.int32, (CHUNK, D), 1)
    for h in range(GROUP):
        a = acc[h * CHUNK : (h + 1) * CHUNK, :]
        den = a[:, D:]
        has = den > 0
        safe = jnp.where(has, den, 1.0)
        mixed = jnp.where(has, a[:, :D] / safe, 0.0)
        out[:, h * D : (h + 1) * D] = mixed.astype(BF16)
        level = jnp.where(has, top[h * CHUNK : (h + 1) * CHUNK, :] + jnp.log2(safe), NEG)
        stat = jnp.where(lane // 16 == h, level, stat)
    out[:, WIDTH:] = split(stat)


def split(stat):
    lane = lax.broadcasted_iota(jnp.int32, stat.shape, 1) % 16
    high = stat.astype(BF16).astype(F32)
    rest = stat - high
    middle = rest.astype(BF16).astype(F32)
    return jnp.where(lane == 0, high, jnp.where(lane == 1, middle, rest - middle)).astype(BF16)


def chunk_attention(step, offset, query, keys, values):
    n = GROUP * CHUNK
    block = 1024
    return pl.pallas_call(
        functools.partial(chunk_kernel, step, block),
        out_shape=jax.ShapeDtypeStruct((CHUNK, MSG), BF16),
        in_specs=[SM, VM, VM, VM],
        out_specs=VM,
        scratch_shapes=[
            pltpu.VMEM((n, D), BF16),
            pltpu.VMEM((n, D), F32),
            pltpu.VMEM((n, 2 * D), F32),
            pltpu.VMEM((n, block), F32),
            pltpu.VMEM((n, block), F32),
        ],
        compiler_params=params(24),
        cost_estimate=cost(5),
    )(offset, query, keys, values)


def merge_kernel(last, *refs):
    parts, out = refs[:-1], refs[-1]
    r = lax.broadcasted_iota(jnp.int32, (D, WIDTH), 0)
    l = lax.broadcasted_iota(jnp.int32, (D, WIDTH), 1)
    spread = jnp.where((r // 16 == l // D) & (r % 16 < 3), 1.0, 0.0).astype(BF16)
    levels = [jnp.dot(p[:, WIDTH:], spread, preferred_element_type=F32) for p in parts]
    best = functools.reduce(jnp.maximum, levels)
    weights = [jnp.exp2(v - best) for v in levels]
    total = functools.reduce(jnp.add, weights)
    mixed = sum(w * p[:, :WIDTH].astype(F32) for w, p in zip(weights, parts))
    out[:, :WIDTH] = (mixed / total).astype(BF16)
    if not last:
        level = best + jnp.log2(total)
        lane = lax.broadcasted_iota(jnp.int32, (level.shape[0], D), 1)
        stat = jnp.zeros((level.shape[0], D), F32)
        for h in range(GROUP):
            stat = jnp.where(lane // 16 == h, level[:, h * D : (h + 1) * D], stat)
        out[:, WIDTH:] = split(stat)


def merge(parts, last):
    n = parts[0].shape[0]
    return pl.pallas_call(
        functools.partial(merge_kernel, last),
        out_shape=jax.ShapeDtypeStruct((n, WIDTH if last else MSG), BF16),
        in_specs=[VM] * len(parts),
        out_specs=VM,
        compiler_params=params(16),
        cost_estimate=cost(1),
    )(*parts)


def decode_kernel(lengths, query, fresh, cache, out, rows):
    r = pl.program_id(0)
    length = lengths[r]
    heads = cache.shape[3] // D
    full = query[0].astype(F32)
    for h in range(heads * GROUP):
        rows[2 * h : 2 * h + 2, :] = full[:, h * D : (h + 1) * D]
    n = 2 * GROUP
    span = cache.shape[2]
    for g in range(heads):
        lanes = slice(g * D, (g + 1) * D)
        q = rows[g * n : (g + 1) * n, :]
        far = nt(q.astype(BF16), cache[0, 0, :, lanes]) * SCALE2
        ok = lax.broadcasted_iota(jnp.int32, (n, span), 1) < length
        far = jnp.where(ok, far, NEG)
        near_keys = fresh[0, 0, :, lanes].astype(F32)
        near_values = fresh[1, 0, :, lanes].astype(F32)
        second = lax.broadcasted_iota(jnp.int32, (n, 1), 0) % 2 == 1
        s0 = jnp.sum(q * near_keys[0:1, :], axis=1, keepdims=True) * SCALE2
        s1 = jnp.sum(q * near_keys[1:2, :], axis=1, keepdims=True) * SCALE2
        s1 = jnp.where(second, s1, NEG)
        best = jnp.maximum(jnp.max(far, axis=1, keepdims=True), jnp.maximum(s0, s1))
        w = jnp.where(ok, jnp.exp2(far - best), 0.0)
        w0 = jnp.exp2(s0 - best)
        w1 = jnp.where(second, jnp.exp2(s1 - best), 0.0)
        total = jnp.sum(w, axis=1, keepdims=True) + w0 + w1
        mixed = jnp.dot(w.astype(BF16), cache[1, 0, :, lanes], preferred_element_type=F32)
        mixed = mixed + w0.astype(BF16).astype(F32) * near_values[0:1, :]
        mixed = mixed + w1.astype(BF16).astype(F32) * near_values[1:2, :]
        rows[g * n : (g + 1) * n, :] = mixed / total
    for h in range(heads * GROUP):
        out[0, :, h * D : (h + 1) * D] = rows[2 * h : 2 * h + 2, :].astype(BF16)


def decode(lengths, query, fresh, cache):
    count, _, width = query.shape
    span, lanes = cache.shape[2:]
    return pl.pallas_call(
        decode_kernel,
        grid=(count,),
        out_shape=jax.ShapeDtypeStruct(query.shape, BF16),
        in_specs=[
            SM,
            pl.BlockSpec((1, 2, width), lambda r: (r, 0, 0)),
            pl.BlockSpec((2, 1, 2, lanes), lambda r: (0, r, 0, 0)),
            pl.BlockSpec((2, 1, span, lanes), lambda r: (0, r, 0, 0)),
        ],
        out_specs=pl.BlockSpec((1, 2, width), lambda r: (r, 0, 0)),
        scratch_shapes=[pltpu.VMEM((width // D * 2, D), F32)],
        compiler_params=params(16),
        cost_estimate=cost(4),
    )(lengths, query, fresh, cache)


def pick_kernel(table, c0, c1, c2, c3, out):
    y, x, c = place()
    pool = lax.axis_index("pool")
    out[...] = jnp.zeros(out.shape, F32)
    for e, ref in enumerate((c0, c1, c2, c3)):
        for d in range(SIDE):
            shard = ((y + 4 - e) % 4 * 4 + (x + 4 - d) % 4) * 2 + c
            for half in range(2):
                group = table[shard * 2 + half]
                home = group // 2

                @pl.when(home // 2 == y * 4 + x)
                def _():
                    page = ref[d * PIECE : (d + 1) * PIECE, WIDTH:].astype(F32)
                    far_core = jnp.where(home % 2 == c, 0, 2)
                    far_pool = jnp.where(group % 2 == pool, 0, 1)
                    out[far_core + far_pool] = page[half * 8 : half * 8 + 8, :]


def deliver(table, chunks):
    picked = pl.pallas_call(
        pick_kernel,
        out_shape=jax.ShapeDtypeStruct((4, 8, 2 * D), F32),
        in_specs=[SM] + [VM] * 4,
        out_specs=VM,
        compiler_params=params(16),
        cost_estimate=cost(1),
    )(table, *chunks)
    whole = picked[:2] + moved(picked[2:], dc=1)
    whole = whole.astype(BF16)
    theirs = lax.ppermute(whole[1], "pool", [(0, 1), (1, 0)])
    pool = lax.axis_index("pool")
    lo = jnp.where(pool == 0, whole[0], theirs)
    hi = jnp.where(pool == 0, theirs, whole[0])
    return jnp.stack(
        [
            jnp.concatenate([lo[:, :D], hi[:, :D]], axis=1),
            jnp.concatenate([lo[:, D:], hi[:, D:]], axis=1),
        ]
    )


def local(
    stretch_query,
    stretch_key_value,
    cache_kv,
    stretch_offset,
    page_table,
    decode_fresh_query,
    decode_fresh_key_value,
    decode_row_cache,
    row_lengths,
):
    other_cache = moved(cache_kv, dc=1)
    other_near = moved(stretch_key_value, dc=1)
    own = jnp.concatenate([stretch_query, stretch_key_value[0], stretch_key_value[1]], axis=1)
    pieces = [own] + [moved(own, dx=d) for d in (1, 2, 3)]
    decode_context = decode(
        row_lengths, decode_fresh_query, decode_fresh_key_value, decode_row_cache
    )
    chunk = jnp.concatenate(pieces, axis=0)
    chunks = [chunk] + [moved(chunk, dy=e) for e in (1, 2, 3)]
    keys, values = prepare(
        stretch_offset, cache_kv, other_cache, stretch_key_value, other_near
    )
    partial = {}
    for e in (1, 3, 2, 0):
        result = chunk_attention(e, stretch_offset, chunks[e], keys, values)
        partial[e] = moved(result, dy=4 - e) if e else result
    group_page_slots = deliver(page_table, chunks)
    rows = merge([partial[e] for e in (0, 1, 3, 2)], False)
    back = [rows[:PIECE]]
    for d in (1, 2, 3):
        back.append(moved(rows[d * PIECE : (d + 1) * PIECE], dx=4 - d))
    prefill_context = merge(back, True)
    return (prefill_context, decode_context, group_page_slots)


def solution(mesh):
    return jax.shard_map(
        local,
        mesh=mesh,
        in_specs=(
            P("ctx", ("tp", "pool")),
            P(None, "ctx", ("tp", "pool")),
            P(None, "ctx", ("tp", "pool")),
            P(),
            P(),
            P(("ctx", "pool"), None, "tp"),
            P(None, ("ctx", "pool"), None, "tp"),
            P(None, ("ctx", "pool"), None, "tp"),
            P(("ctx", "pool")),
        ),
        out_specs=(
            P("ctx", ("tp", "pool")),
            P(("ctx", "pool"), None, "tp"),
            P(None, ("ctx", "pool"), "tp"),
        ),
        check_vma=False,
    )
```

```python
import functools

import jax
import jax.numpy as jnp
from jax import lax
from jax.experimental import pallas as pl
from jax.experimental.pallas import tpu as pltpu
from jax.sharding import Mesh
from jax.sharding import PartitionSpec as P

D = 128
SCALE2 = D ** (-0.5) * 1.4426950408889634
NEG = -1e30
SIDE = 4
PIECE = 16
CHUNK = SIDE * PIECE
GROUP = 8
WIDTH = GROUP * D
MSG = WIDTH + D
CTX = ("y", "x", "core")
F32 = jnp.float32
BF16 = jnp.bfloat16
VM = pl.BlockSpec(memory_space=pltpu.VMEM)
HB = pl.BlockSpec(memory_space=pl.ANY)
SM = pl.BlockSpec(memory_space=pltpu.SMEM)


def place():
    return lax.axis_index("y"), lax.axis_index("x"), lax.axis_index("core")


def moved(value, dy=0, dx=0, dc=0):
    pairs = []
    for y in range(4):
        for x in range(4):
            for c in range(2):
                target = ((y + dy) % 4 * 4 + (x + dx) % 4) * 2 + (c + dc) % 2
                pairs.append(((y * 4 + x) * 2 + c, target))
    return lax.ppermute(value, CTX, pairs)


def params(mib):
    return pltpu.CompilerParams(vmem_limit_bytes=mib << 20)


def cost(us):
    return pl.CostEstimate(flops=int(us * 1.1e9), bytes_accessed=0, transcendentals=0)


def nt(a, b):
    return lax.dot_general(a, b, (((1,), (1,)), ((), ())), preferred_element_type=F32)


def pack_kernel(query, near, out):
    out[:, :WIDTH] = query[...]
    out[:, WIDTH : WIDTH + D] = near[0]
    out[:, WIDTH + D :] = near[1]


def pack(query, near):
    return pl.pallas_call(
        pack_kernel,
        out_shape=jax.ShapeDtypeStruct((PIECE, WIDTH + 2 * D), BF16),
        in_specs=[pl.BlockSpec(), pl.BlockSpec()],
        out_specs=VM,
        compiler_params=params(60),
        cost_estimate=cost(0.3),
    )(query, near)


def stack_kernel(count, *refs):
    out = refs[-1]
    for d in range(SIDE):
        out[d * PIECE : (d + 1) * PIECE, :] = refs[d][...]


def stack(pieces, after):
    return pl.pallas_call(
        functools.partial(stack_kernel, len(after)),
        out_shape=jax.ShapeDtypeStruct((CHUNK, pieces[0].shape[1]), BF16),
        in_specs=[VM] * SIDE + [HB] * len(after),
        out_specs=VM,
        compiler_params=params(16),
        cost_estimate=cost(0.4),
    )(*pieces, *after)


def prepare_kernel(offset, own, other, own_near, other_near, keys, values):
    y, x, c = place()
    span = own.shape[1]
    valid = offset[0] - (y * 4 + x) * 2 * span
    first = jnp.where(c == 0, own[0, 0:16, :].astype(F32), other[0, 0:16, :].astype(F32))[0:1, :]
    for part, (ref, base) in enumerate(((own, c * span), (other, (1 - c) * span))):
        rows = pl.ds(part * span, span)

        @pl.when(valid >= base + span)
        def _():
            keys[rows, :] = ref[0]
            values[rows, 0:D] = ref[1]
            values[rows, D:] = jnp.ones((span, D), BF16)

        @pl.when(valid < base + span)
        def _():
            ok = lax.broadcasted_iota(jnp.int32, (span, D), 0) + base < valid
            keys[rows, :] = jnp.where(ok, ref[0].astype(F32), first).astype(BF16)
            values[rows, 0:D] = jnp.where(ok, ref[1].astype(F32), 0.0).astype(BF16)
            values[rows, D:] = jnp.where(ok, 1.0, 0.0).astype(BF16)

    end = 2 * span
    keys[end : end + 16, :] = own_near[0]
    keys[end + 16 : end + 32, :] = other_near[0]
    keys[end + 32 : end + D, :] = jnp.zeros((D - 32, D), BF16)
    values[end : end + 16, 0:D] = own_near[1]
    values[end + 16 : end + 32, 0:D] = other_near[1]
    values[end + 32 : end + D, 0:D] = jnp.zeros((D - 32, D), BF16)
    values[end : end + D, D:] = jnp.ones((D, D), BF16)


def prepare(offset, own, other, own_near, other_near):
    rows = 2 * own.shape[1] + D
    return pl.pallas_call(
        prepare_kernel,
        out_shape=(
            jax.ShapeDtypeStruct((rows, D), BF16),
            jax.ShapeDtypeStruct((rows, 2 * D), BF16),
        ),
        in_specs=[SM, VM, VM, VM, VM],
        out_specs=(VM, VM),
        compiler_params=params(24),
        cost_estimate=cost(1.5),
    )(offset, own, other, own_near, other_near)


def chunk_kernel(step, turn, offset, query, keys, values, *refs):
    out, rows, low, high = refs[-4:]
    if turn is None:
        chunk_body(step, offset, query, keys, values, out, rows, low, high)
        return
    pool = lax.axis_index("pool")

    @pl.when(pool == turn)
    def _():
        chunk_body(step, offset, query, keys, values, out, rows, low, high)

    if turn == 1:

        @pl.when(pool != turn)
        def _():
            out[...] = refs[0][...]


def chunk_body(step, offset, query, keys, values, out, rows, low, high):
    y, x, c = place()
    n = GROUP * CHUNK
    far = keys.shape[0] - D
    half = far // 2
    chip = (y * 4 + x) * 2
    for h in range(GROUP):
        rows[h * CHUNK : (h + 1) * CHUNK, :] = query[:, h * D : (h + 1) * D]
    low[...] = nt(rows[...], keys[0:half, :])
    score = nt(rows[...], keys[far : far + D, :]) * SCALE2
    high[...] = nt(rows[...], keys[half:far, :])
    line = lax.broadcasted_iota(jnp.int32, (n, D), 0) % CHUNK
    lane = lax.broadcasted_iota(jnp.int32, (n, D), 1)
    token = line % PIECE
    for d in range(SIDE):
        start = (((y + 4 - step) % 4 * 4 + (x + 4 - d) % 4) * 2 + c) * PIECE
        token = token + jnp.where(line // PIECE == d, start, 0)
    key = jnp.where(lane < 16, lane + (chip + c) * PIECE, lane - 16 + (chip + 1 - c) * PIECE)
    ok = (key <= token) & (lane < 32)
    score = jnp.where(ok, score, NEG)
    tops = [jnp.max(score, axis=1, keepdims=True)]
    weight = jnp.where(ok, jnp.exp2(score - tops[0]), 0.0).astype(BF16)
    sums = [jnp.dot(weight, values[far : far + D, :], preferred_element_type=F32)]
    for ref, begin in ((low, 0), (high, half)):
        s = ref[...]
        top = jnp.max(s, axis=1, keepdims=True) * SCALE2
        weight = jnp.exp2(s * SCALE2 - top).astype(BF16)
        sums.append(
            jnp.dot(weight, values[begin : begin + half, :], preferred_element_type=F32)
        )
        tops.append(jnp.where(offset[0] > chip * half, top, NEG))
    best = functools.reduce(jnp.maximum, tops)
    acc = sum(a * jnp.exp2(t - best) for a, t in zip(sums, tops))
    stat = jnp.zeros((CHUNK, D), F32)
    lane = lax.broadcasted_iota(jnp.int32, (CHUNK, D), 1)
    for h in range(GROUP):
        part = slice(h * CHUNK, (h + 1) * CHUNK)
        den = acc[part, D:]
        has = den > 0
        safe = jnp.where(has, den, 1.0)
        out[:, h * D : (h + 1) * D] = (acc[part, :D] / safe).astype(BF16)
        level = jnp.where(has, best[part, :] + jnp.log2(safe), NEG)
        stat = jnp.where(lane // 16 == h, level, stat)
    out[:, WIDTH:] = split(stat)


def split(stat):
    lane = lax.broadcasted_iota(jnp.int32, stat.shape, 1) % 16
    high = stat.astype(BF16).astype(F32)
    rest = stat - high
    middle = rest.astype(BF16).astype(F32)
    return jnp.where(lane == 0, high, jnp.where(lane == 1, middle, rest - middle)).astype(BF16)


def chunk_attention(step, turn, weight, offset, query, keys, values, earlier, after):
    n = GROUP * CHUNK
    half = (keys.shape[0] - D) // 2
    return pl.pallas_call(
        functools.partial(chunk_kernel, step, turn),
        out_shape=jax.ShapeDtypeStruct((CHUNK, MSG), BF16),
        in_specs=[SM, VM, VM, VM] + [VM] * len(earlier) + [HB] * len(after),
        out_specs=VM,
        scratch_shapes=[
            pltpu.VMEM((n, D), BF16),
            pltpu.VMEM((n, half), F32),
            pltpu.VMEM((n, half), F32),
        ],
        compiler_params=params(32),
        cost_estimate=cost(weight),
    )(offset, query, keys, values, *earlier, *after)


def merge_kernel(last, *refs):
    parts, outs = refs[:SIDE], refs[SIDE:]
    r = lax.broadcasted_iota(jnp.int32, (D, WIDTH), 0)
    l = lax.broadcasted_iota(jnp.int32, (D, WIDTH), 1)
    spread = jnp.where((r // 16 == l // D) & (r % 16 < 3), 1.0, 0.0).astype(BF16)
    levels = [jnp.dot(p[:, WIDTH:], spread, preferred_element_type=F32) for p in parts]
    best = functools.reduce(jnp.maximum, levels)
    weights = [jnp.exp2(v - best) for v in levels]
    total = functools.reduce(jnp.add, weights)
    mixed = sum(w * p[:, :WIDTH].astype(F32) for w, p in zip(weights, parts))
    mixed = (mixed / total).astype(BF16)
    for d, out in enumerate(outs):
        out[:, :WIDTH] = mixed[d * PIECE : (d + 1) * PIECE, :]
    if not last:
        level = best + jnp.log2(total)
        lane = lax.broadcasted_iota(jnp.int32, (level.shape[0], D), 1)
        stat = jnp.zeros((level.shape[0], D), F32)
        for h in range(GROUP):
            stat = jnp.where(lane // 16 == h, level[:, h * D : (h + 1) * D], stat)
        stat = split(stat)
        for d, out in enumerate(outs):
            out[:, WIDTH:] = stat[d * PIECE : (d + 1) * PIECE, :]


def merge(parts, last):
    shape = jax.ShapeDtypeStruct((PIECE, WIDTH if last else MSG), BF16)
    return pl.pallas_call(
        functools.partial(merge_kernel, last),
        out_shape=shape if last else (shape,) * SIDE,
        in_specs=[VM] * len(parts),
        out_specs=VM if last else (VM,) * SIDE,
        compiler_params=params(16),
        cost_estimate=cost(1),
    )(*parts)


def decode_kernel(lengths, query, fresh, cache, out, rows):
    r = pl.program_id(0)
    length = lengths[r]
    heads = cache.shape[3] // D
    full = query[0].astype(F32)
    for h in range(heads * GROUP):
        rows[2 * h : 2 * h + 2, :] = full[:, h * D : (h + 1) * D]
    n = 2 * GROUP
    span = cache.shape[2]
    for g in range(heads):
        lanes = slice(g * D, (g + 1) * D)
        q = rows[g * n : (g + 1) * n, :]
        far = nt(q.astype(BF16), cache[0, 0, :, lanes]) * SCALE2
        ok = lax.broadcasted_iota(jnp.int32, (n, span), 1) < length
        far = jnp.where(ok, far, NEG)
        near_keys = fresh[0, 0, :, lanes].astype(F32)
        near_values = fresh[1, 0, :, lanes].astype(F32)
        second = lax.broadcasted_iota(jnp.int32, (n, 1), 0) % 2 == 1
        s0 = jnp.sum(q * near_keys[0:1, :], axis=1, keepdims=True) * SCALE2
        s1 = jnp.sum(q * near_keys[1:2, :], axis=1, keepdims=True) * SCALE2
        s1 = jnp.where(second, s1, NEG)
        best = jnp.maximum(jnp.max(far, axis=1, keepdims=True), jnp.maximum(s0, s1))
        w = jnp.where(ok, jnp.exp2(far - best), 0.0)
        w0 = jnp.exp2(s0 - best)
        w1 = jnp.where(second, jnp.exp2(s1 - best), 0.0)
        total = jnp.sum(w, axis=1, keepdims=True) + w0 + w1
        mixed = jnp.dot(w.astype(BF16), cache[1, 0, :, lanes], preferred_element_type=F32)
        mixed = mixed + w0.astype(BF16).astype(F32) * near_values[0:1, :]
        mixed = mixed + w1.astype(BF16).astype(F32) * near_values[1:2, :]
        rows[g * n : (g + 1) * n, :] = mixed / total
    for h in range(heads * GROUP):
        out[0, :, h * D : (h + 1) * D] = rows[2 * h : 2 * h + 2, :].astype(BF16)


def decode(lengths, query, fresh, cache):
    count, _, width = query.shape
    span, lanes = cache.shape[2:]
    return pl.pallas_call(
        decode_kernel,
        grid=(count,),
        out_shape=jax.ShapeDtypeStruct(query.shape, BF16),
        in_specs=[
            SM,
            pl.BlockSpec((1, 2, width), lambda r: (r, 0, 0)),
            pl.BlockSpec((2, 1, 2, lanes), lambda r: (0, r, 0, 0)),
            pl.BlockSpec((2, 1, span, lanes), lambda r: (0, r, 0, 0)),
        ],
        out_specs=pl.BlockSpec((1, 2, width), lambda r: (r, 0, 0)),
        scratch_shapes=[pltpu.VMEM((width // D * 2, D), F32)],
        compiler_params=params(60),
        cost_estimate=cost(4),
    )(lengths, query, fresh, cache)


def pick_kernel(table, c0, c1, c2, c3, *refs):
    keep, give = refs[-2:]
    y, x, c = place()
    pool = lax.axis_index("pool")
    keep[...] = jnp.zeros(keep.shape, F32)
    give[...] = jnp.zeros(give.shape, F32)
    for e, ref in enumerate((c0, c1, c2, c3)):
        for d in range(SIDE):
            shard = ((y + 4 - e) % 4 * 4 + (x + 4 - d) % 4) * 2 + c
            for half in range(2):
                group = table[shard * 2 + half]

                @pl.when(group // 4 == y * 4 + x)
                def _():
                    page = ref[d * PIECE : (d + 1) * PIECE, WIDTH:].astype(F32)
                    page = page[half * 8 : half * 8 + 8, :]
                    slot = jnp.where(group // 2 % 2 == c, 0, 1)

                    @pl.when(group % 2 == pool)
                    def _():
                        keep[slot] = page

                    @pl.when(group % 2 != pool)
                    def _():
                        give[slot] = page


def pick(table, chunks, after):
    shape = jax.ShapeDtypeStruct((2, 8, 2 * D), F32)
    return pl.pallas_call(
        pick_kernel,
        out_shape=(shape, shape),
        in_specs=[SM] + [VM] * 4 + [HB] * len(after),
        out_specs=(VM, VM),
        compiler_params=params(16),
        cost_estimate=cost(1),
    )(table, *chunks, *after)


def same_kernel(value, after, out):
    out[...] = value[...]


def after_kernel(value, after):
    return pl.pallas_call(
        same_kernel,
        out_shape=jax.ShapeDtypeStruct(value.shape, value.dtype),
        in_specs=[VM, HB],
        out_specs=VM,
        compiler_params=params(16),
        cost_estimate=cost(0.3),
    )(value, after)


def join_kernel(keep, up, down, after, near, far):
    first = lax.axis_index("pool") == 0
    for slot, out in enumerate((near, far)):
        for part in range(2):
            lanes = slice(part * D, (part + 1) * D)
            mine = keep[slot, :, lanes]
            theirs = jnp.where(first, down[slot, :, lanes], up[slot, :, lanes])
            out[part, :, :D] = jnp.where(first, mine, theirs)
            out[part, :, D:] = jnp.where(first, theirs, mine)


def join(keep, up, down, after):
    shape = jax.ShapeDtypeStruct((2, 8, 2 * D), F32)
    return pl.pallas_call(
        join_kernel,
        out_shape=(shape, shape),
        in_specs=[VM, VM, VM, HB],
        out_specs=(VM, VM),
        compiler_params=params(16),
        cost_estimate=cost(0.3),
    )(keep, up, down, after)


def either_kernel(near, far, out):
    out[...] = (near[...] + far[...]).astype(BF16)


def either(near, far):
    return pl.pallas_call(
        either_kernel,
        out_shape=jax.ShapeDtypeStruct(near.shape, BF16),
        in_specs=[VM, VM],
        out_specs=VM,
        compiler_params=params(16),
        cost_estimate=cost(0.3),
    )(near, far)


def local(
    stretch_query,
    stretch_key_value,
    cache_kv,
    stretch_offset,
    page_table,
    decode_fresh_query,
    decode_fresh_key_value,
    decode_row_cache,
    row_lengths,
):
    other_cache = moved(cache_kv, dc=1)
    other_near = moved(stretch_key_value, dc=1)
    own = pack(stretch_query, stretch_key_value)
    pieces = [own] + [moved(own, dx=d) for d in (1, 2, 3)]
    decode_context = decode(
        row_lengths, decode_fresh_query, decode_fresh_key_value, decode_row_cache
    )
    keys, values = prepare(
        stretch_offset, cache_kv, other_cache, stretch_key_value, other_near
    )
    chunk = stack(pieces, [decode_context, keys])
    chunks = [chunk] + [moved(chunk, dy=e) for e in (1, 2, 3)]

    def attend(e, turn, earlier, after, weight=5):
        return chunk_attention(
            e, turn, weight, stretch_offset, chunks[e], keys, values, earlier, after
        )

    one = attend(1, None, [], [])
    one_back = moved(one, dy=3)
    keep, give = pick(page_table, chunks, [one])
    down = lax.ppermute(give, "pool", [(1, 0)])
    three = attend(3, 0, [], [keep], 0.05)
    two = attend(2, 0, [], [three], 0.05)
    up = lax.ppermute(after_kernel(give, two), "pool", [(0, 1)])
    three = attend(3, 1, [three], [two, down])
    three_back = moved(three, dy=1)
    two = attend(2, 1, [two], [three], 0.05)
    two_back = moved(two, dy=2)
    zero = attend(0, None, [], [two, up])
    rows = merge([zero, one_back, three_back, two_back], False)
    back = [rows[0]] + [moved(rows[d], dx=4 - d) for d in (1, 2, 3)]
    near, far = join(keep, up, down, rows[0])
    group_page_slots = either(near, moved(far, dc=1))
    prefill_context = merge(back, True)
    return (prefill_context, decode_context, group_page_slots)


def solution(mesh):
    tp, pool = mesh.shape["tp"], mesh.shape["pool"]
    split_mesh = Mesh(mesh.devices.reshape(4, 4, 2, tp, pool), (*CTX, "tp", "pool"))
    return jax.shard_map(
        local,
        mesh=split_mesh,
        in_specs=(
            P(CTX, ("tp", "pool")),
            P(None, CTX, ("tp", "pool")),
            P(None, CTX, ("tp", "pool")),
            P(),
            P(),
            P((*CTX, "pool"), None, "tp"),
            P(None, (*CTX, "pool"), None, "tp"),
            P(None, (*CTX, "pool"), None, "tp"),
            P((*CTX, "pool")),
        ),
        out_specs=(
            P(CTX, ("tp", "pool")),
            P((*CTX, "pool"), None, "tp"),
            P(None, (*CTX, "pool"), "tp"),
        ),
        check_vma=False,
    )
```

```python
import functools

import jax
import jax.numpy as jnp
from jax import lax
from jax.experimental import pallas as pl
from jax.experimental.pallas import tpu as pltpu
from jax.sharding import Mesh
from jax.sharding import PartitionSpec as P

D = 128
SCALE2 = D ** (-0.5) * 1.4426950408889634
NEG = -1e30
SIDE = 4
PIECE = 16
CHUNK = SIDE * PIECE
GROUP = 8
WIDTH = GROUP * D
MSG = WIDTH + D
CTX = ("y", "x", "core")
F32 = jnp.float32
BF16 = jnp.bfloat16
VM = pl.BlockSpec(memory_space=pltpu.VMEM)
HB = pl.BlockSpec(memory_space=pl.ANY)
SM = pl.BlockSpec(memory_space=pltpu.SMEM)


def place():
    return lax.axis_index("y"), lax.axis_index("x"), lax.axis_index("core")


def moved(value, dy=0, dx=0, dc=0):
    pairs = []
    for y in range(4):
        for x in range(4):
            for c in range(2):
                target = ((y + dy) % 4 * 4 + (x + dx) % 4) * 2 + (c + dc) % 2
                pairs.append(((y * 4 + x) * 2 + c, target))
    return lax.ppermute(value, CTX, pairs)


def params(mib):
    return pltpu.CompilerParams(vmem_limit_bytes=mib << 20)


def cost(us):
    return pl.CostEstimate(flops=int(us * 1.1e9), bytes_accessed=0, transcendentals=0)


def nt(a, b):
    return lax.dot_general(a, b, (((1,), (1,)), ((), ())), preferred_element_type=F32)


def pack_kernel(query, near, out):
    out[:, :WIDTH] = query[...]
    out[:, WIDTH : WIDTH + D] = near[0]
    out[:, WIDTH + D :] = near[1]


def pack(query, near):
    return pl.pallas_call(
        pack_kernel,
        out_shape=jax.ShapeDtypeStruct((PIECE, WIDTH + 2 * D), BF16),
        in_specs=[VM, VM],
        out_specs=VM,
        compiler_params=params(16),
        cost_estimate=cost(0.3),
    )(query, near)


def stack_kernel(count, *refs):
    out = refs[-1]
    for d in range(SIDE):
        out[d * PIECE : (d + 1) * PIECE, :] = refs[d][...]


def stack(pieces, after, token):
    return pl.pallas_call(
        functools.partial(stack_kernel, len(after)),
        out_shape=jax.ShapeDtypeStruct((CHUNK, pieces[0].shape[1]), BF16),
        in_specs=[VM] * SIDE + [HB] * len(after) + [SM],
        out_specs=VM,
        compiler_params=params(16),
        cost_estimate=cost(0.4),
    )(*pieces, *after, token)


def prepare_kernel(offset, own, other, own_near, other_near, after, keys, values):
    y, x, c = place()
    span = own.shape[1]
    valid = offset[0] - (y * 4 + x) * 2 * span
    first = jnp.where(c == 0, own[0, 0:16, :].astype(F32), other[0, 0:16, :].astype(F32))[0:1, :]
    for part, (ref, base) in enumerate(((own, c * span), (other, (1 - c) * span))):
        rows = pl.ds(part * span, span)

        @pl.when(valid >= base + span)
        def _():
            keys[rows, :] = ref[0]
            values[rows, 0:D] = ref[1]
            values[rows, D:] = jnp.ones((span, D), BF16)

        @pl.when(valid < base + span)
        def _():
            ok = lax.broadcasted_iota(jnp.int32, (span, D), 0) + base < valid
            keys[rows, :] = jnp.where(ok, ref[0].astype(F32), first).astype(BF16)
            values[rows, 0:D] = jnp.where(ok, ref[1].astype(F32), 0.0).astype(BF16)
            values[rows, D:] = jnp.where(ok, 1.0, 0.0).astype(BF16)

    end = 2 * span
    keys[end : end + 16, :] = own_near[0]
    keys[end + 16 : end + 32, :] = other_near[0]
    keys[end + 32 : end + D, :] = jnp.zeros((D - 32, D), BF16)
    values[end : end + 16, 0:D] = own_near[1]
    values[end + 16 : end + 32, 0:D] = other_near[1]
    values[end + 32 : end + D, 0:D] = jnp.zeros((D - 32, D), BF16)
    values[end : end + D, D:] = jnp.ones((D, D), BF16)


def prepare(offset, own, other, own_near, other_near, after):
    rows = 2 * own.shape[1] + D
    return pl.pallas_call(
        prepare_kernel,
        out_shape=(
            jax.ShapeDtypeStruct((rows, D), BF16),
            jax.ShapeDtypeStruct((rows, 2 * D), BF16),
        ),
        in_specs=[SM, VM, VM, VM, VM, HB],
        out_specs=(VM, VM),
        compiler_params=params(24),
        cost_estimate=cost(1.5),
    )(offset, own, other, own_near, other_near, after)


def chunk_kernel(step, turn, offset, query, keys, values, *refs):
    out, rows, low, high = refs[-4:]
    if turn is None:
        chunk_body(step, offset, query, keys, values, out, rows, low, high)
        return
    pool = lax.axis_index("pool")

    @pl.when(pool == turn)
    def _():
        chunk_body(step, offset, query, keys, values, out, rows, low, high)

    if turn == 1:

        @pl.when(pool != turn)
        def _():
            out[...] = refs[0][...]


def chunk_body(step, offset, query, keys, values, out, rows, low, high):
    y, x, c = place()
    n = GROUP * CHUNK
    far = keys.shape[0] - D
    half = far // 2
    chip = (y * 4 + x) * 2
    for h in range(GROUP):
        rows[h * CHUNK : (h + 1) * CHUNK, :] = query[:, h * D : (h + 1) * D]
    low[...] = nt(rows[...], keys[0:half, :])
    score = nt(rows[...], keys[far : far + D, :]) * SCALE2
    high[...] = nt(rows[...], keys[half:far, :])
    line = lax.broadcasted_iota(jnp.int32, (n, D), 0) % CHUNK
    lane = lax.broadcasted_iota(jnp.int32, (n, D), 1)
    token = line % PIECE
    for d in range(SIDE):
        start = (((y + 4 - step) % 4 * 4 + (x + 4 - d) % 4) * 2 + c) * PIECE
        token = token + jnp.where(line // PIECE == d, start, 0)
    key = jnp.where(lane < 16, lane + (chip + c) * PIECE, lane - 16 + (chip + 1 - c) * PIECE)
    ok = (key <= token) & (lane < 32)
    score = jnp.where(ok, score, NEG)
    tops = [jnp.max(score, axis=1, keepdims=True)]
    weight = jnp.where(ok, jnp.exp2(score - tops[0]), 0.0).astype(BF16)
    sums = [jnp.dot(weight, values[far : far + D, :], preferred_element_type=F32)]
    for ref, begin in ((low, 0), (high, half)):
        s = ref[...]
        top = jnp.max(s, axis=1, keepdims=True) * SCALE2
        weight = jnp.exp2(s * SCALE2 - top).astype(BF16)
        sums.append(
            jnp.dot(weight, values[begin : begin + half, :], preferred_element_type=F32)
        )
        tops.append(jnp.where(offset[0] > chip * half, top, NEG))
    best = functools.reduce(jnp.maximum, tops)
    acc = sum(a * jnp.exp2(t - best) for a, t in zip(sums, tops))
    stat = jnp.zeros((CHUNK, D), F32)
    lane = lax.broadcasted_iota(jnp.int32, (CHUNK, D), 1)
    for h in range(GROUP):
        part = slice(h * CHUNK, (h + 1) * CHUNK)
        den = acc[part, D:]
        has = den > 0
        safe = jnp.where(has, den, 1.0)
        out[:, h * D : (h + 1) * D] = (acc[part, :D] / safe).astype(BF16)
        level = jnp.where(has, best[part, :] + jnp.log2(safe), NEG)
        stat = jnp.where(lane // 16 == h, level, stat)
    out[:, WIDTH:] = split(stat)


def split(stat):
    lane = lax.broadcasted_iota(jnp.int32, stat.shape, 1) % 16
    high = stat.astype(BF16).astype(F32)
    rest = stat - high
    middle = rest.astype(BF16).astype(F32)
    return jnp.where(lane == 0, high, jnp.where(lane == 1, middle, rest - middle)).astype(BF16)


def chunk_attention(step, turn, weight, offset, query, keys, values, earlier, after):
    n = GROUP * CHUNK
    half = (keys.shape[0] - D) // 2
    return pl.pallas_call(
        functools.partial(chunk_kernel, step, turn),
        out_shape=jax.ShapeDtypeStruct((CHUNK, MSG), BF16),
        in_specs=[SM, VM, VM, VM] + [VM] * len(earlier) + [HB] * len(after),
        out_specs=VM,
        scratch_shapes=[
            pltpu.VMEM((n, D), BF16),
            pltpu.VMEM((n, half), F32),
            pltpu.VMEM((n, half), F32),
        ],
        compiler_params=params(32),
        cost_estimate=cost(weight),
    )(offset, query, keys, values, *earlier, *after)


def merge_kernel(last, *refs):
    parts, outs = refs[:SIDE], refs[SIDE:]
    r = lax.broadcasted_iota(jnp.int32, (D, WIDTH), 0)
    l = lax.broadcasted_iota(jnp.int32, (D, WIDTH), 1)
    spread = jnp.where((r // 16 == l // D) & (r % 16 < 3), 1.0, 0.0).astype(BF16)
    levels = [jnp.dot(p[:, WIDTH:], spread, preferred_element_type=F32) for p in parts]
    best = functools.reduce(jnp.maximum, levels)
    weights = [jnp.exp2(v - best) for v in levels]
    total = functools.reduce(jnp.add, weights)
    mixed = sum(w * p[:, :WIDTH].astype(F32) for w, p in zip(weights, parts))
    mixed = (mixed / total).astype(BF16)
    for d, out in enumerate(outs):
        out[:, :WIDTH] = mixed[d * PIECE : (d + 1) * PIECE, :]
    if not last:
        level = best + jnp.log2(total)
        lane = lax.broadcasted_iota(jnp.int32, (level.shape[0], D), 1)
        stat = jnp.zeros((level.shape[0], D), F32)
        for h in range(GROUP):
            stat = jnp.where(lane // 16 == h, level[:, h * D : (h + 1) * D], stat)
        stat = split(stat)
        for d, out in enumerate(outs):
            out[:, WIDTH:] = stat[d * PIECE : (d + 1) * PIECE, :]


def merge(parts, last):
    shape = jax.ShapeDtypeStruct((PIECE, WIDTH if last else MSG), BF16)
    return pl.pallas_call(
        functools.partial(merge_kernel, last),
        out_shape=shape if last else (shape,) * SIDE,
        in_specs=[VM] * len(parts),
        out_specs=VM if last else (VM,) * SIDE,
        compiler_params=params(16),
        cost_estimate=cost(1),
    )(*parts)


def decode_kernel(r, lengths, query, fresh, cache, *refs):
    out, token, rows = refs[-3:]
    token[0] = 0
    length = lengths[r]
    heads = cache.shape[3] // D
    full = query[0].astype(F32)
    for h in range(heads * GROUP):
        rows[2 * h : 2 * h + 2, :] = full[:, h * D : (h + 1) * D]
    n = 2 * GROUP
    span = cache.shape[2]
    for g in range(heads):
        lanes = slice(g * D, (g + 1) * D)
        q = rows[g * n : (g + 1) * n, :]
        far = nt(q.astype(BF16), cache[0, 0, :, lanes]) * SCALE2
        ok = lax.broadcasted_iota(jnp.int32, (n, span), 1) < length
        far = jnp.where(ok, far, NEG)
        near_keys = fresh[0, 0, :, lanes].astype(F32)
        near_values = fresh[1, 0, :, lanes].astype(F32)
        second = lax.broadcasted_iota(jnp.int32, (n, 1), 0) % 2 == 1
        s0 = jnp.sum(q * near_keys[0:1, :], axis=1, keepdims=True) * SCALE2
        s1 = jnp.sum(q * near_keys[1:2, :], axis=1, keepdims=True) * SCALE2
        s1 = jnp.where(second, s1, NEG)
        best = jnp.maximum(jnp.max(far, axis=1, keepdims=True), jnp.maximum(s0, s1))
        w = jnp.where(ok, jnp.exp2(far - best), 0.0)
        w0 = jnp.exp2(s0 - best)
        w1 = jnp.where(second, jnp.exp2(s1 - best), 0.0)
        total = jnp.sum(w, axis=1, keepdims=True) + w0 + w1
        mixed = jnp.dot(w.astype(BF16), cache[1, 0, :, lanes], preferred_element_type=F32)
        mixed = mixed + w0.astype(BF16).astype(F32) * near_values[0:1, :]
        mixed = mixed + w1.astype(BF16).astype(F32) * near_values[1:2, :]
        rows[g * n : (g + 1) * n, :] = mixed / total
    for h in range(heads * GROUP):
        out[0, :, h * D : (h + 1) * D] = rows[2 * h : 2 * h + 2, :].astype(BF16)


def decode(r, lengths, query, fresh, cache, earlier, after):
    width = query.shape[2]
    span, lanes = cache.shape[2:]
    return pl.pallas_call(
        functools.partial(decode_kernel, r),
        grid=(1,),
        out_shape=(
            jax.ShapeDtypeStruct(query.shape, BF16),
            jax.ShapeDtypeStruct((1,), jnp.int32),
        ),
        in_specs=[
            SM,
            pl.BlockSpec((1, 2, width), lambda i: (r, 0, 0)),
            pl.BlockSpec((2, 1, 2, lanes), lambda i: (0, r, 0, 0)),
            pl.BlockSpec((2, 1, span, lanes), lambda i: (0, r, 0, 0)),
        ]
        + [HB] * (len(earlier) + len(after)),
        out_specs=(pl.BlockSpec((1, 2, width), lambda i: (r, 0, 0)), SM),
        scratch_shapes=[pltpu.VMEM((width // D * 2, D), F32)],
        input_output_aliases={4: 0} if earlier else {},
        compiler_params=params(32 if earlier else 60),
        cost_estimate=cost(2),
    )(lengths, query, fresh, cache, *earlier, *after)


def pick_kernel(table, c0, c1, c2, c3, *refs):
    keep, give = refs[-2:]
    y, x, c = place()
    pool = lax.axis_index("pool")
    keep[...] = jnp.zeros(keep.shape, F32)
    give[...] = jnp.zeros(give.shape, F32)
    for e, ref in enumerate((c0, c1, c2, c3)):
        for d in range(SIDE):
            shard = ((y + 4 - e) % 4 * 4 + (x + 4 - d) % 4) * 2 + c
            for half in range(2):
                group = table[shard * 2 + half]

                @pl.when(group // 4 == y * 4 + x)
                def _():
                    page = ref[d * PIECE : (d + 1) * PIECE, WIDTH:].astype(F32)
                    page = page[half * 8 : half * 8 + 8, :]
                    slot = jnp.where(group // 2 % 2 == c, 0, 1)

                    @pl.when(group % 2 == pool)
                    def _():
                        keep[slot] = page

                    @pl.when(group % 2 != pool)
                    def _():
                        give[slot] = page


def pick(table, chunks, after):
    shape = jax.ShapeDtypeStruct((2, 8, 2 * D), F32)
    return pl.pallas_call(
        pick_kernel,
        out_shape=(shape, shape),
        in_specs=[SM] + [VM] * 4 + [HB] * len(after),
        out_specs=(VM, VM),
        compiler_params=params(16),
        cost_estimate=cost(1),
    )(table, *chunks, *after)


def same_kernel(value, after, out):
    out[...] = value[...]


def after_kernel(value, after):
    return pl.pallas_call(
        same_kernel,
        out_shape=jax.ShapeDtypeStruct(value.shape, value.dtype),
        in_specs=[VM, HB],
        out_specs=VM,
        compiler_params=params(16),
        cost_estimate=cost(0.3),
    )(value, after)


def join_kernel(keep, up, down, after, near, far):
    first = lax.axis_index("pool") == 0
    for slot, out in enumerate((near, far)):
        for part in range(2):
            lanes = slice(part * D, (part + 1) * D)
            mine = keep[slot, :, lanes]
            theirs = jnp.where(first, down[slot, :, lanes], up[slot, :, lanes])
            out[part, :, :D] = jnp.where(first, mine, theirs)
            out[part, :, D:] = jnp.where(first, theirs, mine)


def join(keep, up, down, after):
    shape = jax.ShapeDtypeStruct((2, 8, 2 * D), F32)
    return pl.pallas_call(
        join_kernel,
        out_shape=(shape, shape),
        in_specs=[VM, VM, VM, HB],
        out_specs=(VM, VM),
        compiler_params=params(16),
        cost_estimate=cost(0.3),
    )(keep, up, down, after)


def either_kernel(near, far, out):
    out[...] = (near[...] + far[...]).astype(BF16)


def either(near, far):
    return pl.pallas_call(
        either_kernel,
        out_shape=jax.ShapeDtypeStruct(near.shape, BF16),
        in_specs=[VM, VM],
        out_specs=VM,
        compiler_params=params(16),
        cost_estimate=cost(0.3),
    )(near, far)


def local(
    stretch_query,
    stretch_key_value,
    cache_kv,
    stretch_offset,
    page_table,
    decode_fresh_query,
    decode_fresh_key_value,
    decode_row_cache,
    row_lengths,
):
    other_cache = moved(cache_kv, dc=1)
    other_near = moved(stretch_key_value, dc=1)
    own = pack(stretch_query, stretch_key_value)
    far_piece = moved(own, dx=2)
    pieces = [own, moved(own, dx=1), far_piece, moved(own, dx=3)]
    decode_args = (row_lengths, decode_fresh_query, decode_fresh_key_value, decode_row_cache)
    first_row, token = decode(0, *decode_args, [], [])
    chunk = stack(pieces, [other_near], token)
    chunks = [chunk] + [moved(chunk, dy=e) for e in (1, 2, 3)]
    keys, values = prepare(
        stretch_offset, cache_kv, other_cache, stretch_key_value, other_near, chunk
    )

    def attend(e, turn, earlier, after, weight=5):
        return chunk_attention(
            e, turn, weight, stretch_offset, chunks[e], keys, values, earlier, after
        )

    one = attend(1, None, [], [])
    one_back = moved(one, dy=3)
    keep, give = pick(page_table, chunks, [one])
    down = lax.ppermute(give, "pool", [(1, 0)])
    two = attend(2, 0, [], [keep], 0.05)
    three = attend(3, 0, [], [two], 0.05)
    up = lax.ppermute(after_kernel(give, three), "pool", [(0, 1)])
    two = attend(2, 1, [two], [three, down])
    two_back = moved(two, dy=2)
    three = attend(3, 1, [three], [two], 0.05)
    three_back = moved(three, dy=1)
    zero = attend(0, None, [], [three, up])
    rows = merge([zero, one_back, three_back, two_back], False)
    back = [rows[0]] + [moved(rows[d], dx=4 - d) for d in (2, 1, 3)]
    decode_context, _ = decode(1, *decode_args, [first_row], [rows[0]])
    near, far = join(keep, up, down, rows[0])
    group_page_slots = either(near, moved(far, dc=1))
    prefill_context = merge(back, True)
    return (prefill_context, decode_context, group_page_slots)


def solution(mesh):
    tp, pool = mesh.shape["tp"], mesh.shape["pool"]
    split_mesh = Mesh(mesh.devices.reshape(4, 4, 2, tp, pool), (*CTX, "tp", "pool"))
    return jax.shard_map(
        local,
        mesh=split_mesh,
        in_specs=(
            P(CTX, ("tp", "pool")),
            P(None, CTX, ("tp", "pool")),
            P(None, CTX, ("tp", "pool")),
            P(),
            P(),
            P((*CTX, "pool"), None, "tp"),
            P(None, (*CTX, "pool"), None, "tp"),
            P(None, (*CTX, "pool"), None, "tp"),
            P((*CTX, "pool")),
        ),
        out_specs=(
            P(CTX, ("tp", "pool")),
            P((*CTX, "pool"), None, "tp"),
            P(None, (*CTX, "pool"), "tp"),
        ),
        check_vma=False,
    )
```

```python
import functools

import jax
import jax.numpy as jnp
from jax import lax
from jax.experimental import pallas as pl
from jax.experimental.pallas import tpu as pltpu
from jax.sharding import Mesh
from jax.sharding import PartitionSpec as P

D = 128
SCALE2 = D ** (-0.5) * 1.4426950408889634
NEG = -1e30
SIDE = 4
PIECE = 16
CHUNK = SIDE * PIECE
GROUP = 8
WIDTH = GROUP * D
MSG = WIDTH + D
CTX = ("y", "x", "core")
F32 = jnp.float32
BF16 = jnp.bfloat16
VM = pl.BlockSpec(memory_space=pltpu.VMEM)
HB = pl.BlockSpec(memory_space=pl.ANY)
FAR = pl.BlockSpec(memory_space=pltpu.HBM)
SM = pl.BlockSpec(memory_space=pltpu.SMEM)


def place():
    return lax.axis_index("y"), lax.axis_index("x"), lax.axis_index("core")


def moved(value, dy=0, dx=0, dc=0):
    pairs = []
    for y in range(4):
        for x in range(4):
            for c in range(2):
                target = ((y + dy) % 4 * 4 + (x + dx) % 4) * 2 + (c + dc) % 2
                pairs.append(((y * 4 + x) * 2 + c, target))
    return lax.ppermute(value, CTX, pairs)


def params(mib):
    return pltpu.CompilerParams(vmem_limit_bytes=mib << 20)


def cost(us):
    return pl.CostEstimate(flops=int(us * 1.1e9), bytes_accessed=0, transcendentals=0)


def nt(a, b):
    return lax.dot_general(a, b, (((1,), (1,)), ((), ())), preferred_element_type=F32)


def pack_kernel(query, near, out, sems):
    copies = [
        pltpu.make_async_copy(query, out.at[:, :WIDTH], sems.at[0]),
        pltpu.make_async_copy(near.at[0], out.at[:, WIDTH : WIDTH + D], sems.at[1]),
        pltpu.make_async_copy(near.at[1], out.at[:, WIDTH + D :], sems.at[2]),
    ]
    for copy in copies:
        copy.start()
    for copy in copies:
        copy.wait()


def pack(query, near):
    return pl.pallas_call(
        pack_kernel,
        out_shape=pltpu.VMEM((PIECE, WIDTH + 2 * D), BF16),
        in_specs=[FAR, FAR],
        out_specs=VM,
        scratch_shapes=[pltpu.SemaphoreType.DMA((3,))],
        compiler_params=params(60),
        cost_estimate=cost(0.3),
    )(query, near)


def stack_kernel(count, *refs):
    out = refs[-1]
    for d in range(SIDE):
        out[d * PIECE : (d + 1) * PIECE, :] = refs[d][...]


def stack(pieces, after):
    return pl.pallas_call(
        functools.partial(stack_kernel, len(after)),
        out_shape=jax.ShapeDtypeStruct((CHUNK, pieces[0].shape[1]), BF16),
        in_specs=[VM] * SIDE + [HB] * len(after),
        out_specs=VM,
        compiler_params=params(16),
        cost_estimate=cost(0.4),
    )(*pieces, *after)


def prepare_kernel(offset, own, other, own_near, other_near, after, keys, values):
    y, x, c = place()
    span = own.shape[1]
    valid = offset[0] - (y * 4 + x) * 2 * span
    first = jnp.where(c == 0, own[0, 0:16, :].astype(F32), other[0, 0:16, :].astype(F32))[0:1, :]
    for part, (ref, base) in enumerate(((own, c * span), (other, (1 - c) * span))):
        rows = pl.ds(part * span, span)

        @pl.when(valid >= base + span)
        def _():
            keys[rows, :] = ref[0]
            values[rows, 0:D] = ref[1]
            values[rows, D:] = jnp.ones((span, D), BF16)

        @pl.when(valid < base + span)
        def _():
            ok = lax.broadcasted_iota(jnp.int32, (span, D), 0) + base < valid
            keys[rows, :] = jnp.where(ok, ref[0].astype(F32), first).astype(BF16)
            values[rows, 0:D] = jnp.where(ok, ref[1].astype(F32), 0.0).astype(BF16)
            values[rows, D:] = jnp.where(ok, 1.0, 0.0).astype(BF16)

    end = 2 * span
    keys[end : end + 16, :] = own_near[0]
    keys[end + 16 : end + 32, :] = other_near[0]
    keys[end + 32 : end + D, :] = jnp.zeros((D - 32, D), BF16)
    values[end : end + 16, 0:D] = own_near[1]
    values[end + 16 : end + 32, 0:D] = other_near[1]
    values[end + 32 : end + D, 0:D] = jnp.zeros((D - 32, D), BF16)
    values[end : end + D, D:] = jnp.ones((D, D), BF16)


def prepare(offset, own, other, own_near, other_near, after):
    rows = 2 * own.shape[1] + D
    return pl.pallas_call(
        prepare_kernel,
        out_shape=(
            jax.ShapeDtypeStruct((rows, D), BF16),
            jax.ShapeDtypeStruct((rows, 2 * D), BF16),
        ),
        in_specs=[SM, VM, VM, VM, VM, HB],
        out_specs=(VM, VM),
        compiler_params=params(24),
        cost_estimate=cost(1.5),
    )(offset, own, other, own_near, other_near, after)


def chunk_kernel(step, turn, offset, query, keys, values, *refs):
    out, rows, low, high = refs[-4:]
    if turn is None:
        chunk_body(step, offset, query, keys, values, out, rows, low, high)
        return
    pool = lax.axis_index("pool")

    @pl.when(pool == turn)
    def _():
        chunk_body(step, offset, query, keys, values, out, rows, low, high)

    if turn == 1:

        @pl.when(pool != turn)
        def _():
            out[...] = refs[0][...]


def chunk_body(step, offset, query, keys, values, out, rows, low, high):
    y, x, c = place()
    n = GROUP * CHUNK
    far = keys.shape[0] - D
    half = far // 2
    chip = (y * 4 + x) * 2
    for h in range(GROUP):
        rows[h * CHUNK : (h + 1) * CHUNK, :] = query[:, h * D : (h + 1) * D]
    low[...] = nt(rows[...], keys[0:half, :])
    score = nt(rows[...], keys[far : far + D, :]) * SCALE2
    high[...] = nt(rows[...], keys[half:far, :])
    line = lax.broadcasted_iota(jnp.int32, (n, D), 0) % CHUNK
    lane = lax.broadcasted_iota(jnp.int32, (n, D), 1)
    token = line % PIECE
    for d in range(SIDE):
        start = (((y + 4 - step) % 4 * 4 + (x + 4 - d) % 4) * 2 + c) * PIECE
        token = token + jnp.where(line // PIECE == d, start, 0)
    key = jnp.where(lane < 16, lane + (chip + c) * PIECE, lane - 16 + (chip + 1 - c) * PIECE)
    ok = (key <= token) & (lane < 32)
    score = jnp.where(ok, score, NEG)
    tops = [jnp.max(score, axis=1, keepdims=True)]
    weight = jnp.where(ok, jnp.exp2(score - tops[0]), 0.0).astype(BF16)
    sums = [jnp.dot(weight, values[far : far + D, :], preferred_element_type=F32)]
    for ref, begin in ((low, 0), (high, half)):
        s = ref[...]
        top = jnp.max(s, axis=1, keepdims=True) * SCALE2
        weight = jnp.exp2(s * SCALE2 - top).astype(BF16)
        sums.append(
            jnp.dot(weight, values[begin : begin + half, :], preferred_element_type=F32)
        )
        tops.append(jnp.where(offset[0] > chip * half, top, NEG))
    best = functools.reduce(jnp.maximum, tops)
    acc = sum(a * jnp.exp2(t - best) for a, t in zip(sums, tops))
    stat = jnp.zeros((CHUNK, D), F32)
    lane = lax.broadcasted_iota(jnp.int32, (CHUNK, D), 1)
    for h in range(GROUP):
        part = slice(h * CHUNK, (h + 1) * CHUNK)
        den = acc[part, D:]
        has = den > 0
        safe = jnp.where(has, den, 1.0)
        out[:, h * D : (h + 1) * D] = (acc[part, :D] / safe).astype(BF16)
        level = jnp.where(has, best[part, :] + jnp.log2(safe), NEG)
        stat = jnp.where(lane // 16 == h, level, stat)
    out[:, WIDTH:] = split(stat)


def split(stat):
    lane = lax.broadcasted_iota(jnp.int32, stat.shape, 1) % 16
    high = stat.astype(BF16).astype(F32)
    rest = stat - high
    middle = rest.astype(BF16).astype(F32)
    return jnp.where(lane == 0, high, jnp.where(lane == 1, middle, rest - middle)).astype(BF16)


def chunk_attention(step, turn, weight, offset, query, keys, values, earlier, after):
    n = GROUP * CHUNK
    half = (keys.shape[0] - D) // 2
    return pl.pallas_call(
        functools.partial(chunk_kernel, step, turn),
        out_shape=jax.ShapeDtypeStruct((CHUNK, MSG), BF16),
        in_specs=[SM, VM, VM, VM] + [VM] * len(earlier) + [HB] * len(after),
        out_specs=VM,
        scratch_shapes=[
            pltpu.VMEM((n, D), BF16),
            pltpu.VMEM((n, half), F32),
            pltpu.VMEM((n, half), F32),
        ],
        compiler_params=params(32),
        cost_estimate=cost(weight),
    )(offset, query, keys, values, *earlier, *after)


def merge_kernel(last, *refs):
    parts, outs = refs[:SIDE], refs[SIDE:]
    r = lax.broadcasted_iota(jnp.int32, (D, WIDTH), 0)
    l = lax.broadcasted_iota(jnp.int32, (D, WIDTH), 1)
    spread = jnp.where((r // 16 == l // D) & (r % 16 < 3), 1.0, 0.0).astype(BF16)
    levels = [jnp.dot(p[:, WIDTH:], spread, preferred_element_type=F32) for p in parts]
    best = functools.reduce(jnp.maximum, levels)
    weights = [jnp.exp2(v - best) for v in levels]
    total = functools.reduce(jnp.add, weights)
    mixed = sum(w * p[:, :WIDTH].astype(F32) for w, p in zip(weights, parts))
    mixed = (mixed / total).astype(BF16)
    for d, out in enumerate(outs):
        out[:, :WIDTH] = mixed[d * PIECE : (d + 1) * PIECE, :]
    if not last:
        level = best + jnp.log2(total)
        lane = lax.broadcasted_iota(jnp.int32, (level.shape[0], D), 1)
        stat = jnp.zeros((level.shape[0], D), F32)
        for h in range(GROUP):
            stat = jnp.where(lane // 16 == h, level[:, h * D : (h + 1) * D], stat)
        stat = split(stat)
        for d, out in enumerate(outs):
            out[:, WIDTH:] = stat[d * PIECE : (d + 1) * PIECE, :]


def merge(parts, last):
    shape = jax.ShapeDtypeStruct((PIECE, WIDTH if last else MSG), BF16)
    return pl.pallas_call(
        functools.partial(merge_kernel, last),
        out_shape=shape if last else (shape,) * SIDE,
        in_specs=[VM] * len(parts),
        out_specs=VM if last else (VM,) * SIDE,
        compiler_params=params(16),
        cost_estimate=cost(1),
    )(*parts)


def decode_kernel(r, lengths, query, fresh, cache, *refs):
    out, token, rows = refs[-3:]
    token[...] = jnp.zeros(token.shape, F32)
    decode_body(r, lengths, query, fresh, cache, out, rows)


def decode_body(r, lengths, query, fresh, cache, out, rows, values_ready=None):
    length = lengths[r]
    heads = cache.shape[3] // D
    full = query[0].astype(F32)
    for h in range(heads * GROUP):
        rows[2 * h : 2 * h + 2, :] = full[:, h * D : (h + 1) * D]
    n = 2 * GROUP
    span = cache.shape[2]
    for g in range(heads):
        lanes = slice(g * D, (g + 1) * D)
        q = rows[g * n : (g + 1) * n, :]
        far = nt(q.astype(BF16), cache[0, 0, :, lanes]) * SCALE2
        ok = lax.broadcasted_iota(jnp.int32, (n, span), 1) < length
        far = jnp.where(ok, far, NEG)
        near_keys = fresh[0, 0, :, lanes].astype(F32)
        near_values = fresh[1, 0, :, lanes].astype(F32)
        second = lax.broadcasted_iota(jnp.int32, (n, 1), 0) % 2 == 1
        s0 = jnp.sum(q * near_keys[0:1, :], axis=1, keepdims=True) * SCALE2
        s1 = jnp.sum(q * near_keys[1:2, :], axis=1, keepdims=True) * SCALE2
        s1 = jnp.where(second, s1, NEG)
        best = jnp.maximum(jnp.max(far, axis=1, keepdims=True), jnp.maximum(s0, s1))
        w = jnp.where(ok, jnp.exp2(far - best), 0.0)
        w0 = jnp.exp2(s0 - best)
        w1 = jnp.where(second, jnp.exp2(s1 - best), 0.0)
        total = jnp.sum(w, axis=1, keepdims=True) + w0 + w1
        if g == 0 and values_ready is not None:
            values_ready()
        mixed = jnp.dot(w.astype(BF16), cache[1, 0, :, lanes], preferred_element_type=F32)
        mixed = mixed + w0.astype(BF16).astype(F32) * near_values[0:1, :]
        mixed = mixed + w1.astype(BF16).astype(F32) * near_values[1:2, :]
        rows[g * n : (g + 1) * n, :] = mixed / total
    for h in range(heads * GROUP):
        out[0, :, h * D : (h + 1) * D] = rows[2 * h : 2 * h + 2, :].astype(BF16)


def decode(r, lengths, query, fresh, cache, earlier, after):
    width = query.shape[2]
    span, lanes = cache.shape[2:]
    return pl.pallas_call(
        functools.partial(decode_kernel, r),
        grid=(1,),
        out_shape=(jax.ShapeDtypeStruct(query.shape, BF16), pltpu.VMEM((8, D), F32)),
        in_specs=[
            SM,
            pl.BlockSpec((1, 2, width), lambda i: (r, 0, 0)),
            pl.BlockSpec((2, 1, 2, lanes), lambda i: (0, r, 0, 0)),
            pl.BlockSpec((2, 1, span, lanes), lambda i: (0, r, 0, 0)),
            HB,
            HB,
        ],
        out_specs=(pl.BlockSpec((1, 2, width), lambda i: (r, 0, 0)), VM),
        scratch_shapes=[pltpu.VMEM((width // D * 2, D), F32)],
        input_output_aliases={4: 0},
        compiler_params=params(32),
        cost_estimate=cost(2),
    )(lengths, query, fresh, cache, earlier, after)


def decode_first_kernel(
    lengths, query, fresh, cache, out, token, rows, query_at, fresh_at, cache_at, out_at, sems
):
    copies = [
        pltpu.make_async_copy(query, query_at, sems.at[0]),
        pltpu.make_async_copy(fresh, fresh_at, sems.at[1]),
        pltpu.make_async_copy(cache.at[0, 0], cache_at.at[0, 0], sems.at[2]),
        pltpu.make_async_copy(cache.at[1, 0], cache_at.at[1, 0], sems.at[3]),
    ]
    for copy in copies:
        copy.start()
    token[...] = jnp.zeros(token.shape, F32)
    for copy in copies[:3]:
        copy.wait()
    decode_body(0, lengths, query_at, fresh_at, cache_at, out_at, rows, copies[3].wait)
    copy = pltpu.make_async_copy(out_at, out.at[0:1], sems.at[0])
    copy.start()
    copy.wait()


def decode_first(lengths, query, fresh, cache):
    width = query.shape[2]
    span, lanes = cache.shape[2:]
    return pl.pallas_call(
        decode_first_kernel,
        out_shape=(
            jax.ShapeDtypeStruct(query.shape, BF16),
            pltpu.VMEM((8, D), F32),
        ),
        in_specs=[SM, FAR, FAR, FAR],
        out_specs=(FAR, VM),
        scratch_shapes=[
            pltpu.VMEM((width // D * 2, D), F32),
            pltpu.VMEM(query.shape, BF16),
            pltpu.VMEM(fresh.shape, BF16),
            pltpu.VMEM((2, 1, span, lanes), BF16),
            pltpu.VMEM((1, 2, width), BF16),
            pltpu.SemaphoreType.DMA((4,)),
        ],
        compiler_params=params(60),
        cost_estimate=cost(2),
    )(lengths, query, fresh, cache)


def pick_kernel(table, c0, c1, c2, c3, *refs):
    keep, give = refs[-2:]
    y, x, c = place()
    pool = lax.axis_index("pool")
    keep[...] = jnp.zeros(keep.shape, F32)
    give[...] = jnp.zeros(give.shape, F32)
    first = (y * 4 + x) * 4
    found = [jnp.int32(0)] * 4
    for e in range(SIDE):
        for d in range(SIDE):
            shard = ((y + 4 - e) % 4 * 4 + (x + 4 - d) % 4) * 2 + c
            for half in range(2):
                member = table[shard * 2 + half] - first
                number = (e * SIDE + d) * 2 + half + 1
                found = [f + jnp.where(member == t, number, 0) for t, f in enumerate(found)]
    for t, number in enumerate(found):
        slot = jnp.where(t // 2 == c, 0, 1)
        for e, ref in enumerate((c0, c1, c2, c3)):

            @pl.when((number > e * 8) & (number <= e * 8 + 8))
            def _():
                at = number - 1 - e * 8
                start = pl.multiple_of(at // 2 * PIECE, PIECE)
                page = ref[pl.ds(start, PIECE), WIDTH:].astype(F32)
                page = jnp.where(at % 2 == 1, page[8:, :], page[:8, :])

                @pl.when(pool == t % 2)
                def _():
                    keep[slot] = page

                @pl.when(pool != t % 2)
                def _():
                    give[slot] = page


def pick(table, chunks, after):
    shape = jax.ShapeDtypeStruct((2, 8, 2 * D), F32)
    return pl.pallas_call(
        pick_kernel,
        out_shape=(shape, shape),
        in_specs=[SM] + [VM] * 4 + [HB] * len(after),
        out_specs=(VM, VM),
        compiler_params=params(16),
        cost_estimate=cost(1),
    )(table, *chunks, *after)


def same_kernel(value, after, out):
    out[...] = value[...]


def after_kernel(value, after):
    return pl.pallas_call(
        same_kernel,
        out_shape=jax.ShapeDtypeStruct(value.shape, value.dtype),
        in_specs=[VM, HB],
        out_specs=VM,
        compiler_params=params(16),
        cost_estimate=cost(0.3),
    )(value, after)


def join_kernel(keep, up, down, after, near, far):
    first = lax.axis_index("pool") == 0
    for slot, out in enumerate((near, far)):
        for part in range(2):
            lanes = slice(part * D, (part + 1) * D)
            mine = keep[slot, :, lanes]
            theirs = jnp.where(first, down[slot, :, lanes], up[slot, :, lanes])
            out[part, :, :D] = jnp.where(first, mine, theirs)
            out[part, :, D:] = jnp.where(first, theirs, mine)


def join(keep, up, down, after):
    shape = jax.ShapeDtypeStruct((2, 8, 2 * D), F32)
    return pl.pallas_call(
        join_kernel,
        out_shape=(shape, shape),
        in_specs=[VM, VM, VM, HB],
        out_specs=(VM, VM),
        compiler_params=params(16),
        cost_estimate=cost(0.3),
    )(keep, up, down, after)


def either_kernel(near, far, out):
    out[...] = (near[...] + far[...]).astype(BF16)


def either(near, far):
    return pl.pallas_call(
        either_kernel,
        out_shape=jax.ShapeDtypeStruct(near.shape, BF16),
        in_specs=[VM, VM],
        out_specs=VM,
        compiler_params=params(16),
        cost_estimate=cost(0.3),
    )(near, far)


def local(
    stretch_query,
    stretch_key_value,
    cache_kv,
    stretch_offset,
    page_table,
    decode_fresh_query,
    decode_fresh_key_value,
    decode_row_cache,
    row_lengths,
):
    other_cache = moved(cache_kv, dc=1)
    other_near = moved(stretch_key_value, dc=1)
    own = pack(stretch_query, stretch_key_value)
    far_piece = moved(own, dx=2)
    pieces = [own, moved(own, dx=1), far_piece, moved(own, dx=3)]
    decode_args = (row_lengths, decode_fresh_query, decode_fresh_key_value, decode_row_cache)
    first_row, token = decode_first(*decode_args)
    chunk = stack(pieces, [other_near, token])
    chunks = [chunk] + [moved(chunk, dy=e) for e in (1, 2, 3)]
    keys, values = prepare(
        stretch_offset, cache_kv, other_cache, stretch_key_value, other_near, chunk
    )

    def attend(e, turn, earlier, after, weight=5):
        return chunk_attention(
            e, turn, weight, stretch_offset, chunks[e], keys, values, earlier, after
        )

    one = attend(1, None, [], [])
    one_back = moved(one, dy=3)
    keep, give = pick(page_table, chunks, [one])
    two = attend(2, 0, [], [keep], 0.05)
    three = attend(3, 0, [], [two], 0.05)
    up = lax.ppermute(after_kernel(give, three), "pool", [(0, 1)])
    two = attend(2, 1, [two], [three])
    two_back = moved(two, dy=2)
    three = attend(3, 1, [three], [two], 0.05)
    three_back = moved(three, dy=1)
    zero = attend(0, None, [], [three, up])
    down = lax.ppermute(after_kernel(give, zero), "pool", [(1, 0)])
    rows = merge([zero, one_back, three_back, two_back], False)
    back = [rows[0]] + [moved(rows[d], dx=4 - d) for d in (2, 1, 3)]
    decode_context, token = decode(1, *decode_args, first_row, rows[0])
    near, far = join(keep, up, down, back[1])
    group_page_slots = either(near, moved(far, dc=1))
    prefill_context = merge(back, True)
    return (prefill_context, decode_context, group_page_slots)


def solution(mesh):
    tp, pool = mesh.shape["tp"], mesh.shape["pool"]
    split_mesh = Mesh(mesh.devices.reshape(4, 4, 2, tp, pool), (*CTX, "tp", "pool"))
    return jax.shard_map(
        local,
        mesh=split_mesh,
        in_specs=(
            P(CTX, ("tp", "pool")),
            P(None, CTX, ("tp", "pool")),
            P(None, CTX, ("tp", "pool")),
            P(),
            P(),
            P((*CTX, "pool"), None, "tp"),
            P(None, (*CTX, "pool"), None, "tp"),
            P(None, (*CTX, "pool"), None, "tp"),
            P((*CTX, "pool")),
        ),
        out_specs=(
            P(CTX, ("tp", "pool")),
            P((*CTX, "pool"), None, "tp"),
            P(None, (*CTX, "pool"), "tp"),
        ),
        check_vma=False,
    )
```

```python
import functools

import jax
import jax.numpy as jnp
from jax import lax
from jax.experimental import pallas as pl
from jax.experimental.pallas import tpu as pltpu
from jax.sharding import Mesh
from jax.sharding import PartitionSpec as P

D = 128
SCALE2 = D ** (-0.5) * 1.4426950408889634
NEG = -1e30
SIDE = 4
PIECE = 16
CHUNK = SIDE * PIECE
GROUP = 8
WIDTH = GROUP * D
MSG = WIDTH + D
CTX = ("y", "x", "core")
F32 = jnp.float32
BF16 = jnp.bfloat16
VM = pl.BlockSpec(memory_space=pltpu.VMEM)
HB = pl.BlockSpec(memory_space=pl.ANY)
FAR = pl.BlockSpec(memory_space=pltpu.HBM)
SM = pl.BlockSpec(memory_space=pltpu.SMEM)


def place():
    return lax.axis_index("y"), lax.axis_index("x"), lax.axis_index("core")


def moved(value, dy=0, dx=0, dc=0):
    pairs = []
    for y in range(4):
        for x in range(4):
            for c in range(2):
                target = ((y + dy) % 4 * 4 + (x + dx) % 4) * 2 + (c + dc) % 2
                pairs.append(((y * 4 + x) * 2 + c, target))
    return lax.ppermute(value, CTX, pairs)


def params(mib):
    return pltpu.CompilerParams(vmem_limit_bytes=mib << 20)


def cost(us):
    return pl.CostEstimate(flops=int(us * 1.1e9), bytes_accessed=0, transcendentals=0)


def nt(a, b):
    return lax.dot_general(a, b, (((1,), (1,)), ((), ())), preferred_element_type=F32)


def pack_kernel(query, near, out, sems):
    copies = [
        pltpu.make_async_copy(query, out.at[:, :WIDTH], sems.at[0]),
        pltpu.make_async_copy(near.at[0], out.at[:, WIDTH : WIDTH + D], sems.at[1]),
        pltpu.make_async_copy(near.at[1], out.at[:, WIDTH + D :], sems.at[2]),
    ]
    for copy in copies:
        copy.start()
    for copy in copies:
        copy.wait()


def pack(query, near):
    return pl.pallas_call(
        pack_kernel,
        out_shape=pltpu.VMEM((PIECE, WIDTH + 2 * D), BF16),
        in_specs=[FAR, FAR],
        out_specs=VM,
        scratch_shapes=[pltpu.SemaphoreType.DMA((3,))],
        compiler_params=params(60),
        cost_estimate=cost(0.3),
    )(query, near)


def stack_kernel(count, *refs):
    out = refs[-1]
    for d in range(SIDE):
        out[d * PIECE : (d + 1) * PIECE, :] = refs[d][...]


def stack(pieces, after):
    return pl.pallas_call(
        functools.partial(stack_kernel, len(after)),
        out_shape=jax.ShapeDtypeStruct((CHUNK, pieces[0].shape[1]), BF16),
        in_specs=[VM] * SIDE + [HB] * len(after),
        out_specs=VM,
        compiler_params=params(16),
        cost_estimate=cost(0.4),
    )(*pieces, *after)


def prepare_kernel(offset, own, other, own_near, other_near, after, keys, values):
    y, x, c = place()
    span = own.shape[1]
    valid = offset[0] - (y * 4 + x) * 2 * span
    first = jnp.where(c == 0, own[0, 0:16, :].astype(F32), other[0, 0:16, :].astype(F32))[0:1, :]
    for part, (ref, base) in enumerate(((own, c * span), (other, (1 - c) * span))):
        rows = pl.ds(part * span, span)

        @pl.when(valid >= base + span)
        def _():
            keys[rows, :] = ref[0]
            values[rows, 0:D] = ref[1]
            values[rows, D:] = jnp.ones((span, D), BF16)

        @pl.when(valid < base + span)
        def _():
            ok = lax.broadcasted_iota(jnp.int32, (span, D), 0) + base < valid
            keys[rows, :] = jnp.where(ok, ref[0].astype(F32), first).astype(BF16)
            values[rows, 0:D] = jnp.where(ok, ref[1].astype(F32), 0.0).astype(BF16)
            values[rows, D:] = jnp.where(ok, 1.0, 0.0).astype(BF16)

    end = 2 * span
    keys[end : end + 16, :] = own_near[0]
    keys[end + 16 : end + 32, :] = other_near[0]
    keys[end + 32 : end + D, :] = jnp.zeros((D - 32, D), BF16)
    values[end : end + 16, 0:D] = own_near[1]
    values[end + 16 : end + 32, 0:D] = other_near[1]
    values[end + 32 : end + D, 0:D] = jnp.zeros((D - 32, D), BF16)
    values[end : end + D, D:] = jnp.ones((D, D), BF16)


def prepare(offset, own, other, own_near, other_near, after):
    rows = 2 * own.shape[1] + D
    return pl.pallas_call(
        prepare_kernel,
        out_shape=(
            jax.ShapeDtypeStruct((rows, D), BF16),
            jax.ShapeDtypeStruct((rows, 2 * D), BF16),
        ),
        in_specs=[SM, VM, VM, VM, VM, HB],
        out_specs=(VM, VM),
        compiler_params=params(24),
        cost_estimate=cost(1.5),
    )(offset, own, other, own_near, other_near, after)


def chunk_kernel(step, turn, second, offset, query, keys, values, *refs):
    out, rows, low, high = refs[-4:]
    if turn is None:
        chunk_body(step, offset, query, keys, values, out, rows, low, high)
        return
    pool = lax.axis_index("pool")

    @pl.when(pool == turn)
    def _():
        chunk_body(step, offset, query, keys, values, out, rows, low, high)

    if second:

        @pl.when(pool != turn)
        def _():
            out[...] = refs[0][...]


def chunk_body(step, offset, query, keys, values, out, rows, low, high):
    y, x, c = place()
    n = GROUP * CHUNK
    far = keys.shape[0] - D
    half = far // 2
    chip = (y * 4 + x) * 2
    for h in range(GROUP):
        rows[h * CHUNK : (h + 1) * CHUNK, :] = query[:, h * D : (h + 1) * D]
    low[...] = nt(rows[...], keys[0:half, :])
    score = nt(rows[...], keys[far : far + D, :]) * SCALE2
    high[...] = nt(rows[...], keys[half:far, :])
    line = lax.broadcasted_iota(jnp.int32, (n, D), 0) % CHUNK
    lane = lax.broadcasted_iota(jnp.int32, (n, D), 1)
    token = line % PIECE
    for d in range(SIDE):
        start = (((y + 4 - step) % 4 * 4 + (x + 4 - d) % 4) * 2 + c) * PIECE
        token = token + jnp.where(line // PIECE == d, start, 0)
    key = jnp.where(lane < 16, lane + (chip + c) * PIECE, lane - 16 + (chip + 1 - c) * PIECE)
    ok = (key <= token) & (lane < 32)
    score = jnp.where(ok, score, NEG)
    tops = [jnp.max(score, axis=1, keepdims=True)]
    weight = jnp.where(ok, jnp.exp2(score - tops[0]), 0.0).astype(BF16)
    sums = [jnp.dot(weight, values[far : far + D, :], preferred_element_type=F32)]
    for ref, begin in ((low, 0), (high, half)):
        s = ref[...]
        top = jnp.max(s, axis=1, keepdims=True) * SCALE2
        weight = jnp.exp2(s * SCALE2 - top).astype(BF16)
        sums.append(
            jnp.dot(weight, values[begin : begin + half, :], preferred_element_type=F32)
        )
        tops.append(jnp.where(offset[0] > chip * half, top, NEG))
    best = functools.reduce(jnp.maximum, tops)
    acc = sum(a * jnp.exp2(t - best) for a, t in zip(sums, tops))
    stat = jnp.zeros((CHUNK, D), F32)
    lane = lax.broadcasted_iota(jnp.int32, (CHUNK, D), 1)
    for h in range(GROUP):
        part = slice(h * CHUNK, (h + 1) * CHUNK)
        den = acc[part, D:]
        has = den > 0
        safe = jnp.where(has, den, 1.0)
        out[:, h * D : (h + 1) * D] = (acc[part, :D] / safe).astype(BF16)
        level = jnp.where(has, best[part, :] + jnp.log2(safe), NEG)
        stat = jnp.where(lane // 16 == h, level, stat)
    out[:, WIDTH:] = split(stat)


def split(stat):
    lane = lax.broadcasted_iota(jnp.int32, stat.shape, 1) % 16
    high = stat.astype(BF16).astype(F32)
    rest = stat - high
    middle = rest.astype(BF16).astype(F32)
    return jnp.where(lane == 0, high, jnp.where(lane == 1, middle, rest - middle)).astype(BF16)


def chunk_attention(step, turn, weight, offset, query, keys, values, earlier, after):
    n = GROUP * CHUNK
    half = (keys.shape[0] - D) // 2
    return pl.pallas_call(
        functools.partial(chunk_kernel, step, turn, bool(earlier)),
        out_shape=jax.ShapeDtypeStruct((CHUNK, MSG), BF16),
        in_specs=[SM, VM, VM, VM] + [VM] * len(earlier) + [HB] * len(after),
        out_specs=VM,
        scratch_shapes=[
            pltpu.VMEM((n, D), BF16),
            pltpu.VMEM((n, half), F32),
            pltpu.VMEM((n, half), F32),
        ],
        compiler_params=params(32),
        cost_estimate=cost(weight),
    )(offset, query, keys, values, *earlier, *after)


def merge_kernel(last, *refs):
    parts, outs = refs[:SIDE], refs[SIDE:]
    r = lax.broadcasted_iota(jnp.int32, (D, WIDTH), 0)
    l = lax.broadcasted_iota(jnp.int32, (D, WIDTH), 1)
    spread = jnp.where((r // 16 == l // D) & (r % 16 < 3), 1.0, 0.0).astype(BF16)
    levels = [jnp.dot(p[:, WIDTH:], spread, preferred_element_type=F32) for p in parts]
    best = functools.reduce(jnp.maximum, levels)
    weights = [jnp.exp2(v - best) for v in levels]
    total = functools.reduce(jnp.add, weights)
    mixed = sum(w * p[:, :WIDTH].astype(F32) for w, p in zip(weights, parts))
    mixed = (mixed / total).astype(BF16)
    for d, out in enumerate(outs):
        out[:, :WIDTH] = mixed[d * PIECE : (d + 1) * PIECE, :]
    if not last:
        level = best + jnp.log2(total)
        lane = lax.broadcasted_iota(jnp.int32, (level.shape[0], D), 1)
        stat = jnp.zeros((level.shape[0], D), F32)
        for h in range(GROUP):
            stat = jnp.where(lane // 16 == h, level[:, h * D : (h + 1) * D], stat)
        stat = split(stat)
        for d, out in enumerate(outs):
            out[:, WIDTH:] = stat[d * PIECE : (d + 1) * PIECE, :]


def merge(parts, last):
    shape = jax.ShapeDtypeStruct((PIECE, WIDTH if last else MSG), BF16)
    return pl.pallas_call(
        functools.partial(merge_kernel, last),
        out_shape=shape if last else (shape,) * SIDE,
        in_specs=[VM] * len(parts),
        out_specs=VM if last else (VM,) * SIDE,
        compiler_params=params(16),
        cost_estimate=cost(1),
    )(*parts)


def decode_second_kernel(lengths, query, fresh, cache, earlier, after, out, token, rows):
    token[...] = jnp.zeros(token.shape, F32)
    out[0:1] = earlier[...]
    decode_body(1, lengths, query, fresh, cache, out.at[1:2], rows)


def decode_body(r, lengths, query, fresh, cache, out, rows, values_ready=None):
    length = lengths[r]
    heads = cache.shape[3] // D
    full = query[0].astype(F32)
    for h in range(heads * GROUP):
        rows[2 * h : 2 * h + 2, :] = full[:, h * D : (h + 1) * D]
    n = 2 * GROUP
    span = cache.shape[2]
    for g in range(heads):
        lanes = slice(g * D, (g + 1) * D)
        q = rows[g * n : (g + 1) * n, :]
        far = nt(q.astype(BF16), cache[0, 0, :, lanes]) * SCALE2
        ok = lax.broadcasted_iota(jnp.int32, (n, span), 1) < length
        far = jnp.where(ok, far, NEG)
        near_keys = fresh[0, 0, :, lanes].astype(F32)
        near_values = fresh[1, 0, :, lanes].astype(F32)
        second = lax.broadcasted_iota(jnp.int32, (n, 1), 0) % 2 == 1
        s0 = jnp.sum(q * near_keys[0:1, :], axis=1, keepdims=True) * SCALE2
        s1 = jnp.sum(q * near_keys[1:2, :], axis=1, keepdims=True) * SCALE2
        s1 = jnp.where(second, s1, NEG)
        best = jnp.maximum(jnp.max(far, axis=1, keepdims=True), jnp.maximum(s0, s1))
        w = jnp.where(ok, jnp.exp2(far - best), 0.0)
        w0 = jnp.exp2(s0 - best)
        w1 = jnp.where(second, jnp.exp2(s1 - best), 0.0)
        total = jnp.sum(w, axis=1, keepdims=True) + w0 + w1
        if g == 0 and values_ready is not None:
            values_ready()
        mixed = jnp.dot(w.astype(BF16), cache[1, 0, :, lanes], preferred_element_type=F32)
        mixed = mixed + w0.astype(BF16).astype(F32) * near_values[0:1, :]
        mixed = mixed + w1.astype(BF16).astype(F32) * near_values[1:2, :]
        rows[g * n : (g + 1) * n, :] = mixed / total
    for h in range(heads * GROUP):
        out[0, :, h * D : (h + 1) * D] = rows[2 * h : 2 * h + 2, :].astype(BF16)


def decode_second(lengths, query, fresh, cache, earlier, after):
    width = query.shape[2]
    span, lanes = cache.shape[2:]
    return pl.pallas_call(
        decode_second_kernel,
        grid=(1,),
        out_shape=(jax.ShapeDtypeStruct(query.shape, BF16), pltpu.VMEM((8, D), F32)),
        in_specs=[
            SM,
            pl.BlockSpec((1, 2, width), lambda i: (1, 0, 0)),
            pl.BlockSpec((2, 1, 2, lanes), lambda i: (0, 1, 0, 0)),
            pl.BlockSpec((2, 1, span, lanes), lambda i: (0, 1, 0, 0)),
            VM,
            HB,
        ],
        out_specs=(pl.BlockSpec((2, 2, width), lambda i: (0, 0, 0)), VM),
        scratch_shapes=[pltpu.VMEM((width // D * 2, D), F32)],
        compiler_params=params(32),
        cost_estimate=cost(2),
    )(lengths, query, fresh, cache, earlier, after)


def decode_first_kernel(
    lengths, query, fresh, cache, out, token, rows, query_at, fresh_at, cache_at, sems
):
    copies = [
        pltpu.make_async_copy(query, query_at, sems.at[0]),
        pltpu.make_async_copy(fresh, fresh_at, sems.at[1]),
        pltpu.make_async_copy(cache.at[0, 0], cache_at.at[0, 0], sems.at[2]),
        pltpu.make_async_copy(cache.at[1, 0], cache_at.at[1, 0], sems.at[3]),
    ]
    for copy in copies:
        copy.start()
    token[...] = jnp.zeros(token.shape, F32)
    for copy in copies[:3]:
        copy.wait()
    decode_body(0, lengths, query_at, fresh_at, cache_at, out, rows, copies[3].wait)


def decode_first(lengths, query, fresh, cache):
    width = query.shape[2]
    span, lanes = cache.shape[2:]
    return pl.pallas_call(
        decode_first_kernel,
        out_shape=(pltpu.VMEM((1, 2, width), BF16), pltpu.VMEM((8, D), F32)),
        in_specs=[SM, FAR, FAR, FAR],
        out_specs=(VM, VM),
        scratch_shapes=[
            pltpu.VMEM((width // D * 2, D), F32),
            pltpu.VMEM(query.shape, BF16),
            pltpu.VMEM(fresh.shape, BF16),
            pltpu.VMEM((2, 1, span, lanes), BF16),
            pltpu.SemaphoreType.DMA((4,)),
        ],
        compiler_params=params(60),
        cost_estimate=cost(2),
    )(lengths, query, fresh, cache)


def pick_kernel(table, c0, c1, c2, c3, *refs):
    keep, give = refs[-2:]
    y, x, c = place()
    pool = lax.axis_index("pool")
    keep[...] = jnp.zeros(keep.shape, F32)
    give[...] = jnp.zeros(give.shape, F32)
    first = (y * 4 + x) * 4
    found = [jnp.int32(0)] * 4
    for e in range(SIDE):
        for d in range(SIDE):
            shard = ((y + 4 - e) % 4 * 4 + (x + 4 - d) % 4) * 2 + c
            for half in range(2):
                member = table[shard * 2 + half] - first
                number = (e * SIDE + d) * 2 + half + 1
                found = [f + jnp.where(member == t, number, 0) for t, f in enumerate(found)]
    for t, number in enumerate(found):
        slot = jnp.where(t // 2 == c, 0, 1)
        for e, ref in enumerate((c0, c1, c2, c3)):

            @pl.when((number > e * 8) & (number <= e * 8 + 8))
            def _():
                at = number - 1 - e * 8
                start = pl.multiple_of(at // 2 * PIECE, PIECE)
                page = ref[pl.ds(start, PIECE), WIDTH:].astype(F32)
                page = jnp.where(at % 2 == 1, page[8:, :], page[:8, :])

                @pl.when(pool == t % 2)
                def _():
                    keep[slot] = page

                @pl.when(pool != t % 2)
                def _():
                    give[slot] = page


def pick(table, chunks, after):
    shape = jax.ShapeDtypeStruct((2, 8, 2 * D), F32)
    return pl.pallas_call(
        pick_kernel,
        out_shape=(shape, shape),
        in_specs=[SM] + [VM] * 4 + [HB] * len(after),
        out_specs=(VM, VM),
        compiler_params=params(16),
        cost_estimate=cost(1),
    )(table, *chunks, *after)


def same_kernel(value, after, out):
    out[...] = value[...]


def after_kernel(value, after):
    return pl.pallas_call(
        same_kernel,
        out_shape=jax.ShapeDtypeStruct(value.shape, value.dtype),
        in_specs=[VM, HB],
        out_specs=VM,
        compiler_params=params(16),
        cost_estimate=cost(0.3),
    )(value, after)


def join_kernel(keep, up, down, after, near, far):
    first = lax.axis_index("pool") == 0
    for slot, out in enumerate((near, far)):
        for part in range(2):
            lanes = slice(part * D, (part + 1) * D)
            mine = keep[slot, :, lanes]
            theirs = jnp.where(first, down[slot, :, lanes], up[slot, :, lanes])
            out[part, :, :D] = jnp.where(first, mine, theirs)
            out[part, :, D:] = jnp.where(first, theirs, mine)


def join(keep, up, down, after):
    shape = jax.ShapeDtypeStruct((2, 8, 2 * D), F32)
    return pl.pallas_call(
        join_kernel,
        out_shape=(shape, shape),
        in_specs=[VM, VM, VM, HB],
        out_specs=(VM, VM),
        compiler_params=params(16),
        cost_estimate=cost(0.3),
    )(keep, up, down, after)


def either_kernel(near, far, out):
    out[...] = (near[...] + far[...]).astype(BF16)


def either(near, far):
    return pl.pallas_call(
        either_kernel,
        out_shape=jax.ShapeDtypeStruct(near.shape, BF16),
        in_specs=[VM, VM],
        out_specs=VM,
        compiler_params=params(16),
        cost_estimate=cost(0.3),
    )(near, far)


def local(
    stretch_query,
    stretch_key_value,
    cache_kv,
    stretch_offset,
    page_table,
    decode_fresh_query,
    decode_fresh_key_value,
    decode_row_cache,
    row_lengths,
):
    other_cache = moved(cache_kv, dc=1)
    other_near = moved(stretch_key_value, dc=1)
    own = pack(stretch_query, stretch_key_value)
    far_piece = moved(own, dx=2)
    pieces = [own, moved(own, dx=1), far_piece, moved(own, dx=3)]
    decode_args = (row_lengths, decode_fresh_query, decode_fresh_key_value, decode_row_cache)
    first_row, token = decode_first(*decode_args)
    chunk = stack(pieces, [other_near, token])
    chunks = [chunk] + [moved(chunk, dy=e) for e in (1, 2, 3)]
    keys, values = prepare(
        stretch_offset, cache_kv, other_cache, stretch_key_value, other_near, chunk
    )

    def attend(e, turn, earlier, after, weight=5):
        return chunk_attention(
            e, turn, weight, stretch_offset, chunks[e], keys, values, earlier, after
        )

    one = attend(3, None, [], [])
    one_back = moved(one, dy=1)
    keep, give = pick(page_table, chunks, [one])
    two = attend(2, 0, [], [keep], 0.05)
    three = attend(1, 0, [], [two], 0.05)
    up = lax.ppermute(after_kernel(give, three), "pool", [(0, 1)])
    two = attend(2, 1, [two], [three])
    two_back = moved(two, dy=2)
    three = attend(1, 1, [three], [two], 0.05)
    three_back = moved(three, dy=3)
    zero = attend(0, 1, [], [three, up])
    give = after_kernel(give, zero)
    down = lax.ppermute(give, "pool", [(1, 0)])
    zero = attend(0, 0, [zero], [give], 0.05)
    rows = merge([zero, one_back, three_back, two_back], False)
    back = [rows[0]] + [moved(rows[d], dx=4 - d) for d in (2, 3, 1)]
    decode_context, token = decode_second(*decode_args, first_row, rows[0])
    near, far = join(keep, up, down, back[1])
    group_page_slots = either(near, moved(far, dc=1))
    prefill_context = merge(back, True)
    return (prefill_context, decode_context, group_page_slots)


def solution(mesh):
    tp, pool = mesh.shape["tp"], mesh.shape["pool"]
    split_mesh = Mesh(mesh.devices.reshape(4, 4, 2, tp, pool), (*CTX, "tp", "pool"))
    return jax.shard_map(
        local,
        mesh=split_mesh,
        in_specs=(
            P(CTX, ("tp", "pool")),
            P(None, CTX, ("tp", "pool")),
            P(None, CTX, ("tp", "pool")),
            P(),
            P(),
            P((*CTX, "pool"), None, "tp"),
            P(None, (*CTX, "pool"), None, "tp"),
            P(None, (*CTX, "pool"), None, "tp"),
            P((*CTX, "pool")),
        ),
        out_specs=(
            P(CTX, ("tp", "pool")),
            P((*CTX, "pool"), None, "tp"),
            P(None, (*CTX, "pool"), "tp"),
        ),
        check_vma=False,
    )
```

```python
import functools

import jax
import jax.numpy as jnp
from jax import lax
from jax.experimental import pallas as pl
from jax.experimental.pallas import tpu as pltpu
from jax.sharding import Mesh
from jax.sharding import PartitionSpec as P

D = 128
SCALE2 = D ** (-0.5) * 1.4426950408889634
NEG = -1e30
SIDE = 4
PIECE = 16
CHUNK = SIDE * PIECE
GROUP = 8
WIDTH = GROUP * D
MSG = WIDTH + D
CTX = ("y", "x", "core")
F32 = jnp.float32
BF16 = jnp.bfloat16
VM = pl.BlockSpec(memory_space=pltpu.VMEM)
HB = pl.BlockSpec(memory_space=pl.ANY)
FAR = pl.BlockSpec(memory_space=pltpu.HBM)
SM = pl.BlockSpec(memory_space=pltpu.SMEM)


def place():
    return lax.axis_index("y"), lax.axis_index("x"), lax.axis_index("core")


def moved(value, dy=0, dx=0, dc=0):
    pairs = []
    for y in range(4):
        for x in range(4):
            for c in range(2):
                target = ((y + dy) % 4 * 4 + (x + dx) % 4) * 2 + (c + dc) % 2
                pairs.append(((y * 4 + x) * 2 + c, target))
    return lax.ppermute(value, CTX, pairs)


def params(mib):
    return pltpu.CompilerParams(vmem_limit_bytes=mib << 20)


def cost(us):
    return pl.CostEstimate(flops=int(us * 1.1e9), bytes_accessed=0, transcendentals=0)


def nt(a, b):
    return lax.dot_general(a, b, (((1,), (1,)), ((), ())), preferred_element_type=F32)


def pack_kernel(query, near, out, sems):
    copies = [
        pltpu.make_async_copy(query, out.at[:, :WIDTH], sems.at[0]),
        pltpu.make_async_copy(near.at[0], out.at[:, WIDTH : WIDTH + D], sems.at[1]),
        pltpu.make_async_copy(near.at[1], out.at[:, WIDTH + D :], sems.at[2]),
    ]
    for copy in copies:
        copy.start()
    for copy in copies:
        copy.wait()


def pack(query, near):
    return pl.pallas_call(
        pack_kernel,
        out_shape=pltpu.VMEM((PIECE, WIDTH + 2 * D), BF16),
        in_specs=[FAR, FAR],
        out_specs=VM,
        scratch_shapes=[pltpu.SemaphoreType.DMA((3,))],
        compiler_params=params(60),
        cost_estimate=cost(0.3),
    )(query, near)


def stack_kernel(count, *refs):
    out = refs[-1]
    for ref, d in zip(refs, (0, 2, 3, 1)):
        out[d * PIECE : (d + 1) * PIECE, :] = ref[...]


def stack(pieces, after):
    return pl.pallas_call(
        functools.partial(stack_kernel, len(after)),
        out_shape=jax.ShapeDtypeStruct((CHUNK, pieces[0].shape[1]), BF16),
        in_specs=[VM] * SIDE + [HB] * len(after),
        out_specs=VM,
        compiler_params=params(16),
        cost_estimate=cost(0.4),
    )(*pieces, *after)


def prepare_kernel(offset, own, other, own_near, other_near, after, keys, values):
    y, x, c = place()
    span = own.shape[1]
    valid = offset[0] - (y * 4 + x) * 2 * span
    first = jnp.where(c == 0, own[0, 0:16, :].astype(F32), other[0, 0:16, :].astype(F32))[0:1, :]
    for part, (ref, base) in enumerate(((own, c * span), (other, (1 - c) * span))):
        rows = pl.ds(part * span, span)

        @pl.when(valid >= base + span)
        def _():
            keys[rows, :] = ref[0]
            values[rows, 0:D] = ref[1]
            values[rows, D:] = jnp.ones((span, D), BF16)

        @pl.when(valid < base + span)
        def _():
            ok = lax.broadcasted_iota(jnp.int32, (span, D), 0) + base < valid
            keys[rows, :] = jnp.where(ok, ref[0].astype(F32), first).astype(BF16)
            values[rows, 0:D] = jnp.where(ok, ref[1].astype(F32), 0.0).astype(BF16)
            values[rows, D:] = jnp.where(ok, 1.0, 0.0).astype(BF16)

    end = 2 * span
    keys[end : end + 16, :] = own_near[0]
    keys[end + 16 : end + 32, :] = other_near[0]
    keys[end + 32 : end + D, :] = jnp.zeros((D - 32, D), BF16)
    values[end : end + 16, 0:D] = own_near[1]
    values[end + 16 : end + 32, 0:D] = other_near[1]
    values[end + 32 : end + D, 0:D] = jnp.zeros((D - 32, D), BF16)
    values[end : end + D, D:] = jnp.ones((D, D), BF16)


def prepare(offset, own, other, own_near, other_near, after):
    rows = 2 * own.shape[1] + D
    return pl.pallas_call(
        prepare_kernel,
        out_shape=(
            jax.ShapeDtypeStruct((rows, D), BF16),
            jax.ShapeDtypeStruct((rows, 2 * D), BF16),
        ),
        in_specs=[SM, VM, VM, VM, VM, HB],
        out_specs=(VM, VM),
        compiler_params=params(24),
        cost_estimate=cost(1.5),
    )(offset, own, other, own_near, other_near, after)


def chunk_kernel(step, turn, second, offset, query, keys, values, *refs):
    out, rows, low, high = refs[-4:]
    if turn is None:
        chunk_body(step, offset, query, keys, values, out, rows, low, high)
        return
    pool = lax.axis_index("pool")

    @pl.when(pool == turn)
    def _():
        chunk_body(step, offset, query, keys, values, out, rows, low, high)

    if second:

        @pl.when(pool != turn)
        def _():
            out[...] = refs[0][...]


def chunk_body(step, offset, query, keys, values, out, rows, low, high):
    y, x, c = place()
    n = GROUP * CHUNK
    far = keys.shape[0] - D
    half = far // 2
    chip = (y * 4 + x) * 2
    for h in range(GROUP):
        rows[h * CHUNK : (h + 1) * CHUNK, :] = query[:, h * D : (h + 1) * D]
    low[...] = nt(rows[...], keys[0:half, :])
    score = nt(rows[...], keys[far : far + D, :]) * SCALE2
    high[...] = nt(rows[...], keys[half:far, :])
    line = lax.broadcasted_iota(jnp.int32, (n, D), 0) % CHUNK
    lane = lax.broadcasted_iota(jnp.int32, (n, D), 1)
    token = line % PIECE
    for d in range(SIDE):
        start = (((y + 4 - step) % 4 * 4 + (x + 4 - d) % 4) * 2 + c) * PIECE
        token = token + jnp.where(line // PIECE == d, start, 0)
    key = jnp.where(lane < 16, lane + (chip + c) * PIECE, lane - 16 + (chip + 1 - c) * PIECE)
    ok = (key <= token) & (lane < 32)
    score = jnp.where(ok, score, NEG)
    tops = [jnp.max(score, axis=1, keepdims=True)]
    weight = jnp.where(ok, jnp.exp2(score - tops[0]), 0.0).astype(BF16)
    sums = [jnp.dot(weight, values[far : far + D, :], preferred_element_type=F32)]
    for ref, begin in ((low, 0), (high, half)):
        s = ref[...]
        top = jnp.max(s, axis=1, keepdims=True) * SCALE2
        weight = jnp.exp2(s * SCALE2 - top).astype(BF16)
        sums.append(
            jnp.dot(weight, values[begin : begin + half, :], preferred_element_type=F32)
        )
        tops.append(jnp.where(offset[0] > chip * half, top, NEG))
    best = functools.reduce(jnp.maximum, tops)
    acc = sum(a * jnp.exp2(t - best) for a, t in zip(sums, tops))
    stat = jnp.zeros((CHUNK, D), F32)
    lane = lax.broadcasted_iota(jnp.int32, (CHUNK, D), 1)
    for h in range(GROUP):
        part = slice(h * CHUNK, (h + 1) * CHUNK)
        den = acc[part, D:]
        has = den > 0
        safe = jnp.where(has, den, 1.0)
        out[:, h * D : (h + 1) * D] = (acc[part, :D] / safe).astype(BF16)
        level = jnp.where(has, best[part, :] + jnp.log2(safe), NEG)
        stat = jnp.where(lane // 16 == h, level, stat)
    out[:, WIDTH:] = split(stat)


def split(stat):
    lane = lax.broadcasted_iota(jnp.int32, stat.shape, 1) % 16
    high = stat.astype(BF16).astype(F32)
    rest = stat - high
    middle = rest.astype(BF16).astype(F32)
    return jnp.where(lane == 0, high, jnp.where(lane == 1, middle, rest - middle)).astype(BF16)


def chunk_attention(step, turn, weight, offset, query, keys, values, earlier, after):
    n = GROUP * CHUNK
    half = (keys.shape[0] - D) // 2
    return pl.pallas_call(
        functools.partial(chunk_kernel, step, turn, bool(earlier)),
        out_shape=jax.ShapeDtypeStruct((CHUNK, MSG), BF16),
        in_specs=[SM, VM, VM, VM] + [VM] * len(earlier) + [HB] * len(after),
        out_specs=VM,
        scratch_shapes=[
            pltpu.VMEM((n, D), BF16),
            pltpu.VMEM((n, half), F32),
            pltpu.VMEM((n, half), F32),
        ],
        compiler_params=params(32),
        cost_estimate=cost(weight),
    )(offset, query, keys, values, *earlier, *after)


def merge_kernel(last, *refs):
    parts, outs = refs[:SIDE], refs[SIDE:]
    r = lax.broadcasted_iota(jnp.int32, (D, WIDTH), 0)
    l = lax.broadcasted_iota(jnp.int32, (D, WIDTH), 1)
    spread = jnp.where((r // 16 == l // D) & (r % 16 < 3), 1.0, 0.0).astype(BF16)
    levels = [jnp.dot(p[:, WIDTH:], spread, preferred_element_type=F32) for p in parts]
    best = functools.reduce(jnp.maximum, levels)
    weights = [jnp.exp2(v - best) for v in levels]
    total = functools.reduce(jnp.add, weights)
    mixed = sum(w * p[:, :WIDTH].astype(F32) for w, p in zip(weights, parts))
    mixed = (mixed / total).astype(BF16)
    for d, out in enumerate(outs):
        out[:, :WIDTH] = mixed[d * PIECE : (d + 1) * PIECE, :]
    if not last:
        level = best + jnp.log2(total)
        lane = lax.broadcasted_iota(jnp.int32, (level.shape[0], D), 1)
        stat = jnp.zeros((level.shape[0], D), F32)
        for h in range(GROUP):
            stat = jnp.where(lane // 16 == h, level[:, h * D : (h + 1) * D], stat)
        stat = split(stat)
        for d, out in enumerate(outs):
            out[:, WIDTH:] = stat[d * PIECE : (d + 1) * PIECE, :]


def merge(parts, last):
    shape = jax.ShapeDtypeStruct((PIECE, WIDTH if last else MSG), BF16)
    return pl.pallas_call(
        functools.partial(merge_kernel, last),
        out_shape=shape if last else (shape,) * SIDE,
        in_specs=[VM] * len(parts),
        out_specs=VM if last else (VM,) * SIDE,
        compiler_params=params(16),
        cost_estimate=cost(1),
    )(*parts)


def decode_second_kernel(lengths, query, fresh, cache, earlier, after, out, token, rows):
    token[...] = jnp.zeros(token.shape, F32)
    out[0:1] = earlier[...]
    decode_body(1, lengths, query, fresh, cache, out.at[1:2], rows)


def decode_body(r, lengths, query, fresh, cache, out, rows, values_ready=None):
    length = lengths[r]
    heads = cache.shape[3] // D
    full = query[0].astype(F32)
    for h in range(heads * GROUP):
        rows[2 * h : 2 * h + 2, :] = full[:, h * D : (h + 1) * D]
    n = 2 * GROUP
    span = cache.shape[2]
    for g in range(heads):
        lanes = slice(g * D, (g + 1) * D)
        q = rows[g * n : (g + 1) * n, :]
        far = nt(q.astype(BF16), cache[0, 0, :, lanes]) * SCALE2
        ok = lax.broadcasted_iota(jnp.int32, (n, span), 1) < length
        far = jnp.where(ok, far, NEG)
        near_keys = fresh[0, 0, :, lanes].astype(F32)
        near_values = fresh[1, 0, :, lanes].astype(F32)
        second = lax.broadcasted_iota(jnp.int32, (n, 1), 0) % 2 == 1
        s0 = jnp.sum(q * near_keys[0:1, :], axis=1, keepdims=True) * SCALE2
        s1 = jnp.sum(q * near_keys[1:2, :], axis=1, keepdims=True) * SCALE2
        s1 = jnp.where(second, s1, NEG)
        best = jnp.maximum(jnp.max(far, axis=1, keepdims=True), jnp.maximum(s0, s1))
        w = jnp.where(ok, jnp.exp2(far - best), 0.0)
        w0 = jnp.exp2(s0 - best)
        w1 = jnp.where(second, jnp.exp2(s1 - best), 0.0)
        total = jnp.sum(w, axis=1, keepdims=True) + w0 + w1
        if g == 0 and values_ready is not None:
            values_ready()
        mixed = jnp.dot(w.astype(BF16), cache[1, 0, :, lanes], preferred_element_type=F32)
        mixed = mixed + w0.astype(BF16).astype(F32) * near_values[0:1, :]
        mixed = mixed + w1.astype(BF16).astype(F32) * near_values[1:2, :]
        rows[g * n : (g + 1) * n, :] = mixed / total
    for h in range(heads * GROUP):
        out[0, :, h * D : (h + 1) * D] = rows[2 * h : 2 * h + 2, :].astype(BF16)


def decode_second(lengths, query, fresh, cache, earlier, after):
    width = query.shape[2]
    span, lanes = cache.shape[2:]
    return pl.pallas_call(
        decode_second_kernel,
        grid=(1,),
        out_shape=(jax.ShapeDtypeStruct(query.shape, BF16), pltpu.VMEM((8, D), F32)),
        in_specs=[
            SM,
            pl.BlockSpec((1, 2, width), lambda i: (1, 0, 0)),
            pl.BlockSpec((2, 1, 2, lanes), lambda i: (0, 1, 0, 0)),
            pl.BlockSpec((2, 1, span, lanes), lambda i: (0, 1, 0, 0)),
            VM,
            HB,
        ],
        out_specs=(pl.BlockSpec((2, 2, width), lambda i: (0, 0, 0)), VM),
        scratch_shapes=[pltpu.VMEM((width // D * 2, D), F32)],
        compiler_params=params(32),
        cost_estimate=cost(2),
    )(lengths, query, fresh, cache, earlier, after)


def decode_first_kernel(
    lengths, query, fresh, cache, out, token, rows, query_at, fresh_at, cache_at, sems
):
    copies = [
        pltpu.make_async_copy(query, query_at, sems.at[0]),
        pltpu.make_async_copy(fresh, fresh_at, sems.at[1]),
        pltpu.make_async_copy(cache.at[0, 0], cache_at.at[0, 0], sems.at[2]),
        pltpu.make_async_copy(cache.at[1, 0], cache_at.at[1, 0], sems.at[3]),
    ]
    for copy in copies:
        copy.start()
    token[...] = jnp.zeros(token.shape, F32)
    for copy in copies[:3]:
        copy.wait()
    decode_body(0, lengths, query_at, fresh_at, cache_at, out, rows, copies[3].wait)


def decode_first(lengths, query, fresh, cache):
    width = query.shape[2]
    span, lanes = cache.shape[2:]
    return pl.pallas_call(
        decode_first_kernel,
        out_shape=(pltpu.VMEM((1, 2, width), BF16), pltpu.VMEM((8, D), F32)),
        in_specs=[SM, FAR, FAR, FAR],
        out_specs=(VM, VM),
        scratch_shapes=[
            pltpu.VMEM((width // D * 2, D), F32),
            pltpu.VMEM(query.shape, BF16),
            pltpu.VMEM(fresh.shape, BF16),
            pltpu.VMEM((2, 1, span, lanes), BF16),
            pltpu.SemaphoreType.DMA((4,)),
        ],
        compiler_params=params(60),
        cost_estimate=cost(2),
    )(lengths, query, fresh, cache)


def pick_kernel(table, c0, c1, c2, c3, *refs):
    keep, give = refs[-2:]
    y, x, c = place()
    pool = lax.axis_index("pool")
    keep[...] = jnp.zeros(keep.shape, F32)
    give[...] = jnp.zeros(give.shape, F32)
    first = (y * 4 + x) * 4
    found = [jnp.int32(0)] * 4
    for e in range(SIDE):
        for d in range(SIDE):
            shard = ((y + 4 - e) % 4 * 4 + (x + 4 - d) % 4) * 2 + c
            for half in range(2):
                member = table[shard * 2 + half] - first
                number = (e * SIDE + d) * 2 + half + 1
                found = [f + jnp.where(member == t, number, 0) for t, f in enumerate(found)]
    for t, number in enumerate(found):
        slot = jnp.where(t // 2 == c, 0, 1)
        for e, ref in enumerate((c0, c1, c2, c3)):

            @pl.when((number > e * 8) & (number <= e * 8 + 8))
            def _():
                at = number - 1 - e * 8
                start = pl.multiple_of(at // 2 * PIECE, PIECE)
                page = ref[pl.ds(start, PIECE), WIDTH:].astype(F32)
                page = jnp.where(at % 2 == 1, page[8:, :], page[:8, :])

                @pl.when(pool == t % 2)
                def _():
                    keep[slot] = page

                @pl.when(pool != t % 2)
                def _():
                    give[slot] = page


def pick(table, chunks, after):
    shape = jax.ShapeDtypeStruct((2, 8, 2 * D), F32)
    return pl.pallas_call(
        pick_kernel,
        out_shape=(shape, shape),
        in_specs=[SM] + [VM] * 4 + [HB] * len(after),
        out_specs=(VM, VM),
        compiler_params=params(16),
        cost_estimate=cost(1),
    )(table, *chunks, *after)


def same_kernel(value, after, out):
    out[...] = value[...]


def after_kernel(value, after):
    return pl.pallas_call(
        same_kernel,
        out_shape=jax.ShapeDtypeStruct(value.shape, value.dtype),
        in_specs=[VM, HB],
        out_specs=VM,
        compiler_params=params(16),
        cost_estimate=cost(0.3),
    )(value, after)


def join_kernel(keep, up, down, after, near, far):
    first = lax.axis_index("pool") == 0
    for slot, out in enumerate((near, far)):
        for part in range(2):
            lanes = slice(part * D, (part + 1) * D)
            mine = keep[slot, :, lanes]
            theirs = jnp.where(first, down[slot, :, lanes], up[slot, :, lanes])
            out[part, :, :D] = jnp.where(first, mine, theirs)
            out[part, :, D:] = jnp.where(first, theirs, mine)


def join(keep, up, down, after):
    shape = jax.ShapeDtypeStruct((2, 8, 2 * D), F32)
    return pl.pallas_call(
        join_kernel,
        out_shape=(shape, shape),
        in_specs=[VM, VM, VM, HB],
        out_specs=(VM, VM),
        compiler_params=params(16),
        cost_estimate=cost(0.3),
    )(keep, up, down, after)


def either_kernel(near, far, out):
    out[...] = (near[...] + far[...]).astype(BF16)


def either(near, far):
    return pl.pallas_call(
        either_kernel,
        out_shape=jax.ShapeDtypeStruct(near.shape, BF16),
        in_specs=[VM, VM],
        out_specs=VM,
        compiler_params=params(16),
        cost_estimate=cost(0.3),
    )(near, far)


def local(
    stretch_query,
    stretch_key_value,
    cache_kv,
    stretch_offset,
    page_table,
    decode_fresh_query,
    decode_fresh_key_value,
    decode_row_cache,
    row_lengths,
):
    other_cache = moved(cache_kv, dc=1)
    other_near = moved(stretch_key_value, dc=1)
    own = pack(stretch_query, stretch_key_value)
    pieces = [own] + [moved(own, dx=d) for d in (2, 3, 1)]
    decode_args = (row_lengths, decode_fresh_query, decode_fresh_key_value, decode_row_cache)
    first_row, token = decode_first(*decode_args)
    chunk = stack(pieces, [other_near, token])
    chunks = [chunk] + [moved(chunk, dy=e) for e in (1, 2, 3)]
    keys, values = prepare(
        stretch_offset, cache_kv, other_cache, stretch_key_value, other_near, chunk
    )

    def attend(e, turn, earlier, after, weight=5):
        return chunk_attention(
            e, turn, weight, stretch_offset, chunks[e], keys, values, earlier, after
        )

    one = attend(1, None, [], [])
    one_back = moved(one, dy=3)
    keep, give = pick(page_table, chunks, [one])
    two = attend(2, 0, [], [keep], 0.05)
    three = attend(3, 0, [], [two], 0.05)
    up = lax.ppermute(after_kernel(give, three), "pool", [(0, 1)])
    two = attend(2, 1, [two], [three])
    two_back = moved(two, dy=2)
    three = attend(3, 1, [three], [two], 0.05)
    three_back = moved(three, dy=1)
    zero = attend(0, 1, [], [three, up])
    give = after_kernel(give, zero)
    down = lax.ppermute(give, "pool", [(1, 0)])
    zero = attend(0, 0, [zero], [give], 0.05)
    rows = merge([zero, one_back, three_back, two_back], False)
    back = [rows[0]] + [moved(rows[d], dx=4 - d) for d in (2, 3, 1)]
    decode_context, token = decode_second(*decode_args, first_row, rows[0])
    near, far = join(keep, up, down, back[1])
    group_page_slots = either(near, moved(far, dc=1))
    prefill_context = merge(back, True)
    return (prefill_context, decode_context, group_page_slots)


def solution(mesh):
    tp, pool = mesh.shape["tp"], mesh.shape["pool"]
    split_mesh = Mesh(mesh.devices.reshape(4, 4, 2, tp, pool), (*CTX, "tp", "pool"))
    return jax.shard_map(
        local,
        mesh=split_mesh,
        in_specs=(
            P(CTX, ("tp", "pool")),
            P(None, CTX, ("tp", "pool")),
            P(None, CTX, ("tp", "pool")),
            P(),
            P(),
            P((*CTX, "pool"), None, "tp"),
            P(None, (*CTX, "pool"), None, "tp"),
            P(None, (*CTX, "pool"), None, "tp"),
            P((*CTX, "pool")),
        ),
        out_specs=(
            P(CTX, ("tp", "pool")),
            P((*CTX, "pool"), None, "tp"),
            P(None, (*CTX, "pool"), "tp"),
        ),
        check_vma=False,
    )
```
